32 devices in a mesh: groups: 2 (over y), dp: 8 (over z, x), tensor: 2 (over core).
Axes of the slice: x: 2, y: 2, z: 4, core: 2. Of those that a mesh axis runs over, the one named last changes fastest.
Arguments:
- requests: bfloat16 [6144, 8192], P(('groups', 'dp'), 'tensor'), parts along dimension 0, may hold values from -6 to 6
- adapter_index: int32 [6144, 1], P(('groups', 'dp')), parts along dimension 0, may hold values from 0 to 7; in each aligned block of 384 rows (0 to 383, 384 to 767, ...) at most 96 rows name the same one
- storage_slot_index: int32 [16], P('groups'), parts along dimension 0, may hold values from 0 to 7, each once
- key_base_weight: bfloat16 [8192, 1024], P('tensor'), may hold values from -0.0625 to 0.0625
- adapter_down_factor: bfloat16 [16, 8192, 64], P(('groups', 'dp'), 'tensor'), parts along dimension 0, may hold values from -0.0625 to 0.0625
- adapter_up_factor: bfloat16 [16, 64, 1024], P(('groups', 'dp')), parts along dimension 0, may hold values from -0.75 to 0.75
Outputs:
- key_rows: bfloat16 [6144, 1024], P(('groups', 'dp'), 'tensor'), parts along dimension 0
The draws below stay inside these ranges and needn't reach their ends.
There are 2 independent parts, one for each index of `groups`. The reference program is written for one: setup_inputs(seed, part) draws one part's arguments, and reference() takes and returns one part's arrays. A program takes and returns all parts, laid end to end along the dimension named above; an argument that names none is the same for every part. Nothing has to cross between parts.
Inputs may be any that keep to these rules, and one draw needn't show every extreme that they name: `adapter_index`: in each aligned block of 384 rows (the requests of one index of dp) no adapter is named by more than 96 rows, a bound that some block reaches; every adapter is named by some request. `storage_slot_index`: each slot holds exactly one adapter; slot s is stored on index s of dp.
All inputs are finite; a program needn't handle non-finite values.
Results may differ from the reference program's by a relative error of at most 0.001.
Values may be sent and summed in bfloat16 or wider, within the bound.
No kernel may reach another device: no remote copies, remote signals or barrier semaphores. Data moves between devices by JAX's collectives and lax.ppermute only.
A program may use at most 128 MiB of HBM per device.

```python
import math
import jax
import jax.numpy as jnp
import numpy as np
from jax import lax

MODEL_WIDTH = 8192
KEY_WIDTH = 1024
ADAPTER_RANK = 64
REQ_DEV = 384
REQUEST_COUNT = 3072
ADAPTER_COUNT = 8
CAP = 96


def level_of(stream_key, dims, shards, least, largest):
    def one(position, shards_of):
        steps = jax.random.uniform(jax.random.fold_in(jax.random.fold_in(stream_key, 6), position), (shards_of,), jnp.float32, least / len(shards), largest / len(shards))
        return jnp.repeat(jnp.exp(steps), dims[position] // shards_of).reshape((-1,) + (1,) * (len(dims) - position - 1))

    level = one(*shards[0])
    for cut in shards[1:]:
        level = level * one(*cut)
    return level


def routed_block(stream_key, own, number, rows, amount, top, reach, skew):
    order = jax.random.permutation(stream_key, amount)
    crowded, ordinary = shares(amount, rows * top, reach, skew, True), shares(amount, rows * top, reach, skew, False)
    places = jnp.arange(amount)

    def named(sizes, rotation):
        used = int((sizes > 0).sum())
        fixed = max(1, used // 4)
        shifted = fixed + (places - fixed + rotation * (used - fixed)) % max(1, amount - fixed)
        return jnp.zeros((amount,), jnp.int32).at[order[jnp.where(places < fixed, places, shifted)]].set(jnp.asarray(sizes, jnp.int32))

    sizes = jnp.where(number % 4 == 0, named(crowded, number // 4), named(ordinary, number - number // 4 - 1))
    mixed = jax.random.permutation(jax.random.fold_in(own, 3), amount)
    giver, taker = mixed[0:amount // 2 * 2:2], mixed[1:amount // 2 * 2:2]
    margin = jnp.minimum(sizes[giver] - 1, reach - sizes[taker]) // 2
    margin = jnp.where((giver == order[0]) | (taker == order[0]) | (sizes[taker] == 0), 0, jnp.maximum(margin, 0))
    shifted = jax.random.randint(jax.random.fold_in(own, 4), (amount // 2,), 0, 1 << 20) % (margin + 1)
    sizes = sizes.at[giver].add(-shifted).at[taker].add(shifted)
    members = jnp.searchsorted(jnp.cumsum(sizes), jnp.arange(rows * top), side="right").astype(jnp.int32)
    listing = members.reshape(top, rows).T
    listing = listing[jax.random.permutation(jax.random.fold_in(own, 1), rows)]
    rotation = jax.random.randint(jax.random.fold_in(own, 2), (rows, 1), 0, top)
    return jnp.take_along_axis(listing, (jnp.arange(top)[None, :] + rotation) % top, axis=1)


def shares(number_of, total, most, skew, full):
    weights = [(1 << 20) // math.isqrt(rank ** skew) + 1 for rank in range(1, number_of + 1)]
    largest = most if full else min(most, max(-(-total // number_of), total * weights[0] // sum(weights)))
    least = 1 if total - largest >= number_of - 1 else 0
    given, spare = [largest] + [least] * (number_of - 1), total - largest - least * (number_of - 1)
    while spare > 0:
        free = [i for i in range(1, number_of) if given[i] < largest] or [i for i in range(1, number_of) if given[i] < most]
        whole, left = sum([weights[i] for i in free]), spare
        for i in free:
            more = min(most - given[i], max(1, left * weights[i] // whole), spare)
            given[i] = given[i] + more
            spare = spare - more
    return np.array(given)


def bell_draw(own_key, shape, scale, bound, shards=(), held_as=jnp.bfloat16):
    result = scale * jax.random.normal(own_key, shape, jnp.float32)
    if shards:
        result = result * level_of(own_key, shape, shards, -0.22, 0.18)
    return jnp.clip(result, -bound, bound).astype(held_as)


def setup_inputs(seed: int = 0, part: int = 0) -> dict:
    key_of = jax.random.split(jax.random.key(seed), 7)
    part_splits = jax.random.split(jax.random.fold_in(key_of[6], part), 7)
    requests = bell_draw(part_splits[0], (REQUEST_COUNT, MODEL_WIDTH), 1.0, 6.0, ((0, 8), (1, 2)))
    adapter_index_keys = jax.random.split(jax.random.fold_in(part_splits[1], 1), REQUEST_COUNT // REQ_DEV)
    adapter_index_turns = jax.random.permutation(jax.random.fold_in(part_splits[1], 3), REQUEST_COUNT // REQ_DEV)
    adapter_index = jax.vmap(lambda own, number: routed_block(jax.random.fold_in(part_splits[1], 2), own, number, REQ_DEV, ADAPTER_COUNT, 1, CAP, 2))(adapter_index_keys, adapter_index_turns).reshape((REQUEST_COUNT, 1))
    storage_slot_index = jax.random.permutation(part_splits[2], ADAPTER_COUNT).astype(jnp.int32)
    key_base_weight = bell_draw(key_of[3], (MODEL_WIDTH, KEY_WIDTH), MODEL_WIDTH ** -0.5, 0.0625, ((0, 2),))
    adapter_down_factor = bell_draw(part_splits[4], (ADAPTER_COUNT, MODEL_WIDTH, ADAPTER_RANK), MODEL_WIDTH ** -0.5, 0.0625, ((0, 8), (1, 2)))
    adapter_up_factor = bell_draw(part_splits[5], (ADAPTER_COUNT, ADAPTER_RANK, KEY_WIDTH), ADAPTER_RANK ** -0.5, 0.75, ((0, 8),))
    return dict(requests=requests, adapter_index=adapter_index, storage_slot_index=storage_slot_index, key_base_weight=key_base_weight, adapter_down_factor=adapter_down_factor, adapter_up_factor=adapter_up_factor)


def reference(requests, adapter_index, storage_slot_index, key_base_weight, adapter_down_factor, adapter_up_factor):
    base_part = jnp.dot(requests, key_base_weight, preferred_element_type=jnp.float32)
    slots = storage_slot_index[adapter_index[:, 0]].astype(jnp.int32)
    input_blocks = requests.reshape(REQUEST_COUNT // 8, 8, MODEL_WIDTH)
    storage_slot_blocks = slots.reshape(REQUEST_COUNT // 8, 8)

    def adapter_block(factor_couple):
        x_rows, storage_slot_rows = factor_couple
        down_factor_rows = adapter_down_factor[storage_slot_rows].astype(jnp.float32)
        up_factor_rows = adapter_up_factor[storage_slot_rows].astype(jnp.float32)
        down_part = jnp.einsum("td,tdr->tr", x_rows.astype(jnp.float32), down_factor_rows, precision=lax.Precision.HIGHEST)
        return jnp.einsum("tr,trk->tk", down_part, up_factor_rows, precision=lax.Precision.HIGHEST)

    raised_output = lax.map(adapter_block, (input_blocks, storage_slot_blocks)).reshape(REQUEST_COUNT, KEY_WIDTH)
    return (base_part + raised_output).astype(jnp.bfloat16)
```

```python
import jax
import jax.numpy as jnp
from jax import lax
from jax.sharding import PartitionSpec as P

CHUNKS = 2


def ring_of(n):
    if n % 2 == 0 and n <= 16:
        return list(range(0, n, 2)) + list(range(n - 1, 0, -2))
    return list(range(n))


def shards(n, requests, adapter_index, storage_slot_index, key_base_weight, down_factor, up_factor):
    rows, half = requests.shape
    rank = down_factor.shape[2]
    keys = up_factor.shape[2]
    out_keys = keys // 2
    order = ring_of(n)
    place = [order.index(i) for i in range(n)]
    me = lax.axis_index("dp")
    core = lax.axis_index("tensor")

    moves = []
    for j in range(n):
        a, b = order[j], order[(j + 1) % n]
        moves += [(2 * a, 2 * b), (2 * b + 1, 2 * a + 1)]

    table = jnp.arange(storage_slot_index.shape[0], dtype=jnp.int32)
    slot = jnp.sum(
        jnp.where(adapter_index == table[None, :], storage_slot_index[None, :], 0), axis=1, keepdims=True
    )

    a_t = down_factor[0].T
    b_own = lax.dynamic_slice_in_dim(up_factor[0], core * out_keys, out_keys, axis=1)
    own = jnp.concatenate([a_t, b_own], axis=1)
    step_rows = rank // CHUNKS
    held = [[own[c * step_rows : (c + 1) * step_rows] for c in range(CHUNKS)]]
    for _ in range(n - 1):
        held.append([lax.ppermute(h, ("dp", "tensor"), moves) for h in held[-1]])

    w_there = lax.dynamic_slice_in_dim(key_base_weight, (1 - core) * out_keys, out_keys, axis=1)
    w_here = lax.dynamic_slice_in_dim(key_base_weight, core * out_keys, out_keys, axis=1)
    there = jnp.dot(requests, w_there, preferred_element_type=jnp.float32)
    swap = [(0, 1), (1, 0)]
    base = jnp.dot(requests, w_here, preferred_element_type=jnp.float32) + lax.ppermute(there, "tensor", swap)

    pos = jnp.array(place, jnp.int32)[me]
    way = jnp.where(core == 0, -1, 1)
    total = jnp.zeros((rows, rank), jnp.float32)
    origins = []
    for s in range(n):
        origin = jnp.array(order, jnp.int32)[(pos + way * s + n) % n]
        origins.append(origin)
        block = jnp.concatenate([h[:, :half] for h in held[s]], axis=0)
        part = lax.dot_general(
            requests, block, (((1,), (1,)), ((), ())), preferred_element_type=jnp.float32
        )
        total = jnp.where(slot == origin, part, total)
    total = total + lax.ppermute(total, "tensor", swap)

    high = total.astype(jnp.bfloat16)
    rest = total - high.astype(jnp.float32)
    mid = rest.astype(jnp.bfloat16)
    low = (rest - mid.astype(jnp.float32)).astype(jnp.bfloat16)
    b_flat = jnp.concatenate([h[:, half:] for hs in held for h in hs], axis=0)
    lifted = base
    for piece in (low, mid, high):
        wide = jnp.concatenate([jnp.where(slot == o, piece, jnp.bfloat16(0)) for o in origins], axis=1)
        lifted = lifted + jnp.dot(wide, b_flat, preferred_element_type=jnp.float32)
    return lifted.astype(jnp.bfloat16)


def solution(mesh):
    placed = (
        P(("groups", "dp"), "tensor"),
        P(("groups", "dp"), None),
        P("groups"),
        P("tensor", None),
        P(("groups", "dp"), "tensor", None),
        P(("groups", "dp"), None, None),
    )
    n = mesh.shape["dp"]
    return jax.shard_map(
        lambda *a: shards(n, *a),
        mesh=mesh,
        in_specs=placed,
        out_specs=P(("groups", "dp"), "tensor"),
        check_vma=False,
    )
```

```python
import jax
import jax.numpy as jnp
from jax import lax
from jax.sharding import PartitionSpec as P


def ring_of(n):
    if n % 2 == 0 and n <= 16:
        return list(range(0, n, 2)) + list(range(n - 1, 0, -2))
    return list(range(n))


def shards(n, requests, adapter_index, storage_slot_index, key_base_weight, down_factor, up_factor):
    rows, half = requests.shape
    rank = down_factor.shape[2]
    keys = up_factor.shape[2]
    out_keys = keys // 2
    order = ring_of(n)
    place = [order.index(i) for i in range(n)]
    me = lax.axis_index("dp")
    core = lax.axis_index("tensor")

    forth, back = [], []
    for j in range(n):
        a, b = order[j], order[(j + 1) % n]
        forth += [(2 * a, 2 * b), (2 * b + 1, 2 * a + 1)]
        back += [(2 * b, 2 * a), (2 * a + 1, 2 * b + 1)]
    swap = [(0, 1), (1, 0)]

    steps = [[(place[d] - place[s]) * (1 - 2 * c) % n for s in range(n)] for d in range(n) for c in range(2)]
    steps_here = lax.dynamic_index_in_dim(jnp.array(steps, jnp.int32), 2 * me + core, 0, keepdims=False)
    slots = jnp.arange(n, dtype=jnp.int32)
    steps_of = jnp.sum(jnp.where(storage_slot_index[:, None] == slots[None, :], steps_here[None, :], 0), axis=1)
    far = jnp.sum(jnp.where(adapter_index == slots[None, :], steps_of[None, :], 0), axis=1)

    a_t = down_factor[0].T
    b_own = lax.dynamic_slice_in_dim(up_factor[0], core * out_keys, out_keys, axis=1)
    own = jnp.concatenate([a_t, b_own], axis=1)

    w_there = lax.dynamic_slice_in_dim(key_base_weight, (1 - core) * out_keys, out_keys, axis=1)
    w_here = lax.dynamic_slice_in_dim(key_base_weight, core * out_keys, out_keys, axis=1)
    there = jnp.dot(requests, w_there, preferred_element_type=jnp.float32)
    there, own_late = lax.optimization_barrier((there, own))
    here = jnp.dot(requests, w_here, preferred_element_type=jnp.float32)

    pieces = [(0, 0, own)]
    p, q = own, own_late
    for s in range(1, (n - 1) // 2 + 1):
        p = lax.ppermute(p, ("dp", "tensor"), forth)
        q = lax.ppermute(q, ("dp", "tensor"), back)
        if s == 1:
            here, p = lax.optimization_barrier((here, p))
        pieces += [(s, 0, p), (n - s, 0, q)]
    if n % 2 == 0:
        mid = rank // 2
        pieces += [
            (n // 2, 0, lax.ppermute(p[:mid], ("dp", "tensor"), forth)),
            (n // 2, mid, lax.ppermute(q[mid:], ("dp", "tensor"), back)),
        ]

    base = here + lax.ppermute(there, "tensor", swap)

    total = jnp.zeros((rank, rows), jnp.float32)
    for s, first, piece in pieces:
        last = first + piece.shape[0]
        part = lax.dot_general(
            piece[:, :half], requests, (((1,), (1,)), ((), ())), preferred_element_type=jnp.float32
        )
        part = jnp.where((far == s)[None, :], part, total[first:last])
        total = part if first == 0 and last == rank else total.at[first:last].set(part)
    total = total + lax.ppermute(total, "tensor", swap)

    rounded = lax.reduce_precision(total, exponent_bits=8, mantissa_bits=7)
    high = rounded.astype(jnp.bfloat16)
    low = (total - rounded).astype(jnp.bfloat16)
    b_flat = jnp.concatenate([piece[:, half:] for _, _, piece in pieces], axis=0)
    lifted = base
    for part in (low, high):
        wide = jnp.concatenate(
            [
                jnp.where((far == s)[None, :], part[f : f + h.shape[0]], jnp.bfloat16(0))
                for s, f, h in pieces
            ],
            axis=0,
        )
        lifted = lifted + lax.dot_general(
            wide, b_flat, (((0,), (0,)), ((), ())), preferred_element_type=jnp.float32
        )
    return lifted.astype(jnp.bfloat16)


def solution(mesh):
    placed = (
        P(("groups", "dp"), "tensor"),
        P(("groups", "dp"), None),
        P("groups"),
        P("tensor", None),
        P(("groups", "dp"), "tensor", None),
        P(("groups", "dp"), None, None),
    )
    n = mesh.shape["dp"]
    return jax.shard_map(
        lambda *a: shards(n, *a),
        mesh=mesh,
        in_specs=placed,
        out_specs=P(("groups", "dp"), "tensor"),
        check_vma=False,
    )
```

```python
import functools

import jax
import jax.numpy as jnp
from jax import lax
from jax.experimental import pallas as pl
from jax.experimental.pallas import tpu as pltpu
from jax.sharding import PartitionSpec as P

BASE_PARTS = 2
LANES = 128
tie = lax.optimization_barrier
VMEM = pl.BlockSpec(memory_space=pltpu.VMEM)
SMEM = pl.BlockSpec(memory_space=pltpu.SMEM)
HBM = pl.BlockSpec(memory_space=pl.ANY)
SMALL = pl.CostEstimate(flops=1000, bytes_accessed=1000, transcendentals=0)


def ring_of(n):
    if n % 2 == 0 and n <= 16:
        return list(range(0, n, 2)) + list(range(n - 1, 0, -2))
    return list(range(n))


def call(kernel, shape, dtype, in_specs, *args, mib=24, scratch=()):
    return pl.pallas_call(
        kernel,
        in_specs=in_specs,
        out_specs=VMEM,
        out_shape=jax.ShapeDtypeStruct(shape, dtype),
        scratch_shapes=scratch,
        compiler_params=pltpu.CompilerParams(vmem_limit_bytes=mib << 20),
        cost_estimate=SMALL,
    )(*args)


def pack_kernel(half, out_keys, a_ref, b_ref, o_ref, a_sem, b_sem):
    first = pl.multiple_of(lax.axis_index("tensor") * out_keys, out_keys)
    a_copy = pltpu.make_async_copy(a_ref, o_ref.at[:, :half], a_sem)
    b_copy = pltpu.make_async_copy(b_ref.at[:, pl.ds(first, out_keys)], o_ref.at[:, half:], b_sem)
    a_copy.start()
    b_copy.start()
    a_copy.wait()
    b_copy.wait()


def far_kernel(n, index_ref, storage_ref, steps_ref, o_ref):
    row = (2 * lax.axis_index("dp") + lax.axis_index("tensor")) * n
    index = index_ref[...]

    def look(j, far):
        return jnp.where(index == j, steps_ref[row + storage_ref[j]], far)

    far = lax.fori_loop(0, n, look, jnp.zeros_like(index))
    o_ref[...] = jnp.broadcast_to(far, o_ref.shape)


def base_kernel(other, offset, out_keys, x_ref, w_ref, o_ref):
    core = lax.axis_index("tensor")
    core = 1 - core if other else core
    width = o_ref.shape[1]
    first = pl.multiple_of(core * out_keys + offset, width)
    o_ref[...] = jnp.dot(x_ref[...], w_ref[:, pl.ds(first, width)], preferred_element_type=jnp.float32)


def down_kernel(half, s, x_ref, m_ref, far_ref, *rest):
    o_ref = rest[-1]
    part = lax.dot_general(
        x_ref[...], m_ref[:, :half], (((1,), (1,)), ((), ())), preferred_element_type=jnp.float32
    )
    if s is not None:
        kept = rest[0][...] if len(rest) > 1 else 0.0
        o_ref[...] = jnp.where(far_ref[:, : part.shape[1]] == s, part, kept)
    elif len(rest) > 1:
        o_ref[...] = jnp.concatenate([rest[0][...], part], axis=1)
    else:
        o_ref[...] = part


def lift(steps, far_ref, total, b_refs, out_of):
    high = total.astype(jnp.bfloat16)
    low = (total - high.astype(jnp.float32)).astype(jnp.bfloat16)
    rank = total.shape[1]
    far = far_ref[:, :rank]
    out_keys = out_of.shape[1]
    b_all = jnp.concatenate([b[:, b.shape[1] - out_keys :] for b in b_refs], axis=0)
    out = None
    for part in (low, high):
        part = part.astype(jnp.float32)
        wide = jnp.concatenate([jnp.where(far == s, part, 0.0).astype(jnp.bfloat16) for s in steps], axis=1)
        product = jnp.dot(wide, b_all, preferred_element_type=jnp.float32)
        out = product if out is None else out + product
    return out


def up_kernel(steps, parts, far_ref, own_ref, other_ref, there_ref, *rest):
    o_ref = rest[-1]
    lifted = lift(steps, far_ref, own_ref[...] + other_ref[...], rest[parts:-1], o_ref)
    here = jnp.concatenate([h[...] for h in rest[:parts]], axis=1)
    o_ref[...] = here + there_ref[...] + lifted


def last_kernel(steps, far_ref, own_ref, other_ref, base_ref, *rest):
    lifted = lift(steps, far_ref, own_ref[...] + other_ref[...], rest[:-1], rest[-1])
    rest[-1][...] = (base_ref[...] + lifted).astype(jnp.bfloat16)


def shards(n, requests, adapter_index, storage_slot_index, key_base_weight, down_factor, up_factor):
    rows, half = requests.shape
    rank = down_factor.shape[2]
    keys = up_factor.shape[2]
    out_keys = keys // 2
    order = ring_of(n)
    place = [order.index(i) for i in range(n)]

    forth, back = [], []
    for j in range(n):
        a, b = order[j], order[(j + 1) % n]
        forth += [(2 * a, 2 * b), (2 * b + 1, 2 * a + 1)]
        back += [(2 * b, 2 * a), (2 * a + 1, 2 * b + 1)]
    swap = [(0, 1), (1, 0)]
    both = ("dp", "tensor")

    steps = [(place[d] - place[s]) * (1 - 2 * c) % n for d in range(n) for c in range(2) for s in range(n)]

    def base_of(x, other, offset, width):
        kernel = functools.partial(base_kernel, other, offset, out_keys)
        return call(kernel, (rows, width), jnp.float32, [VMEM, VMEM], x, key_base_weight)

    def down_of(x, message, s, *total):
        width = message.shape[0] + (total[0].shape[1] if total and s is None else 0)
        kernel = functools.partial(down_kernel, half, s)
        return call(
            kernel, (rows, width), jnp.float32, [VMEM] * (3 + len(total)), x, message, far, *total, mib=16
        )

    own = call(
        functools.partial(pack_kernel, half, out_keys),
        (rank, half + out_keys),
        jnp.bfloat16,
        [HBM, HBM],
        down_factor[0].T,
        up_factor[0],
        mib=8,
        scratch=[pltpu.SemaphoreType.DMA] * 2,
    )

    there = base_of(requests, True, 0, out_keys)
    far = call(
        functools.partial(far_kernel, n),
        (rows, LANES),
        jnp.int32,
        [VMEM, SMEM, SMEM],
        adapter_index,
        storage_slot_index,
        jnp.array(steps, jnp.int32),
        mib=8,
    )
    total = down_of(requests, own, 0)
    there, total, q = tie((there, total, own))
    from_there = lax.ppermute(there, "tensor", swap)
    here = []
    width = out_keys // BASE_PARTS

    def base_part(x):
        return [base_of(x, False, len(here) * width, width)] if len(here) < BASE_PARTS else []

    p = own
    pieces = [(0, own)]
    waiting = None
    for s in range(1, (n - 1) // 2 + 1):
        p = lax.ppermute(p, both, forth)
        q = lax.ppermute(q, both, back)
        for turn in range(2):
            arrived = q if turn else p
            x = requests
            work = []
            if waiting is not None:
                _, x = tie((waiting[1], requests))
                work.append(down_of(x, waiting[1], waiting[0], total))
            more = base_part(x)
            arrived, *work = tie((arrived, *work, *more))
            here += work[len(work) - len(more) :]
            if waiting is not None:
                total = work[0]
            waiting = (n - s, arrived) if turn else (s, arrived)
            pieces.append(waiting)
            if turn:
                q = arrived
            else:
                p = arrived
    while len(here) < BASE_PARTS:
        here += base_part(requests)

    opposite = n % 2 == 0 and n > 1
    if opposite:
        mid = rank // 2
        p = lax.ppermute(p[:mid], both, forth)
        q = lax.ppermute(q[mid:], both, back)
    if waiting is not None:
        _, x = tie((waiting[1], requests))
        total = down_of(x, waiting[1], waiting[0], total)
    other = lax.ppermute(total, "tensor", swap)
    messages = [m if n <= 16 else m[:, half:] for _, m in pieces]
    base = call(
        functools.partial(up_kernel, [s for s, _ in pieces], BASE_PARTS),
        (rows, out_keys),
        jnp.float32,
        [VMEM] * (4 + BASE_PARTS + len(messages)),
        far,
        total,
        other,
        from_there,
        *here,
        *messages,
        mib=32,
    )
    if not opposite:
        return base.astype(jnp.bfloat16)
    base, p = tie((base, p))
    total = down_of(requests, p, None)
    total, q = tie((total, q))
    total = down_of(requests, q, None, total)
    other = lax.ppermute(total, "tensor", swap)
    return call(
        functools.partial(last_kernel, [n // 2]),
        (rows, out_keys),
        jnp.bfloat16,
        [VMEM] * 6,
        far,
        total,
        other,
        base,
        p,
        q,
        mib=16,
    )


def solution(mesh):
    placed = (
        P(("groups", "dp"), "tensor"),
        P(("groups", "dp"), None),
        P("groups"),
        P("tensor", None),
        P(("groups", "dp"), "tensor", None),
        P(("groups", "dp"), None, None),
    )
    n = mesh.shape["dp"]
    return jax.shard_map(
        functools.partial(shards, n),
        mesh=mesh,
        in_specs=placed,
        out_specs=P(("groups", "dp"), "tensor"),
        check_vma=False,
    )
```

```python
import functools

import jax
import jax.numpy as jnp
from jax import lax
from jax.experimental import pallas as pl
from jax.experimental.pallas import tpu as pltpu
from jax.sharding import PartitionSpec as P

LANES = 128
BASE_STEPS = 8
tie = lax.optimization_barrier
VMEM = pl.BlockSpec(memory_space=pltpu.VMEM)
SMEM = pl.BlockSpec(memory_space=pltpu.SMEM)
HBM = pl.BlockSpec(memory_space=pl.ANY)


def snakes(n):
    return n % 2 == 0 and n <= 16


def ring_of(n):
    if snakes(n):
        return list(range(0, n, 2)) + list(range(n - 1, 0, -2))
    return list(range(n))


def place_in(n, i):
    return jnp.where(i % 2 == 0, i // 2, n - 1 - i // 2) if snakes(n) else i


def call(kernel, outs, in_specs, *args, mib=16, scratch=(), moved=1000):
    shapes = [jax.ShapeDtypeStruct(shape, dtype) for shape, dtype in outs]
    got = pl.pallas_call(
        kernel,
        in_specs=in_specs,
        out_specs=[VMEM] * len(outs),
        out_shape=shapes,
        scratch_shapes=scratch,
        compiler_params=pltpu.CompilerParams(vmem_limit_bytes=mib << 20),
        cost_estimate=pl.CostEstimate(flops=1000, bytes_accessed=moved, transcendentals=0),
    )(*args)
    return got[0] if len(outs) == 1 else got


def pack_kernel(a_ref, b_ref, o_ref, sems):
    rank, half = a_ref.shape
    k_half, b_half = half // 2, o_ref.shape[1] - half // 2
    first = lax.axis_index("tensor") * (2 * b_half)
    copies = []
    for i in range(2):
        rows = pl.ds(i * rank, rank)
        b_first = pl.multiple_of(first + i * b_half, b_half)
        copies += [
            (a_ref.at[:, pl.ds(i * k_half, k_half)], o_ref.at[rows, pl.ds(0, k_half)]),
            (b_ref.at[:, pl.ds(b_first, b_half)], o_ref.at[rows, pl.ds(k_half, b_half)]),
        ]
    copies = [pltpu.make_async_copy(*c, sems.at[i]) for i, c in enumerate(copies)]
    for c in copies:
        c.start()
    for c in copies:
        c.wait()


def far_kernel(n, index_ref, storage_ref, o_ref):
    here = place_in(n, lax.axis_index("dp"))
    way = 1 - 2 * lax.axis_index("tensor")
    index = index_ref[...]

    def look(j, far):
        return jnp.where(index == j, lax.rem((here - place_in(n, storage_ref[j])) * way + n, n), far)

    far = lax.fori_loop(0, n, look, jnp.zeros_like(index))
    o_ref[...] = jnp.broadcast_to(far, o_ref.shape)


def base_kernel(x_hbm, w_hbm, x_ref, there_ref, here_ref, w_ref, x_sems, w_sems):
    depth = x_hbm.shape[1] // BASE_STEPS
    keys = here_ref.shape[1]
    core = lax.axis_index("tensor")
    copies = []
    for i in range(BASE_STEPS):
        k = pl.ds(i * depth, depth)
        copies.append(
            (
                pltpu.make_async_copy(x_hbm.at[:, k], x_ref.at[:, k], x_sems.at[i]),
                pltpu.make_async_copy(w_hbm.at[k, :], w_ref.at[k, :], w_sems.at[i]),
            )
        )
        for c in copies[-1]:
            c.start()
    for i in range(BASE_STEPS):
        k = pl.ds(i * depth, depth)
        for c in copies[i]:
            c.wait()
        for o_ref, side in ((there_ref, 1 - core), (here_ref, core)):
            columns = pl.ds(pl.multiple_of(side * keys, keys), keys)
            product = jnp.dot(x_ref[:, k], w_ref[k, columns], preferred_element_type=jnp.float32)
            o_ref[...] = product if i == 0 else o_ref[...] + product


def down_kernel(s, x_ref, m_ref, far_ref, *rest):
    o_ref = rest[-1]
    rank = o_ref.shape[1]
    k_half = x_ref.shape[1] // 2
    part = None
    for i in range(2):
        product = lax.dot_general(
            x_ref[:, i * k_half : (i + 1) * k_half],
            m_ref[i * rank : (i + 1) * rank, :k_half],
            (((1,), (1,)), ((), ())),
            preferred_element_type=jnp.float32,
        )
        part = product if part is None else part + product
    kept = rest[0][...] if len(rest) > 1 else 0.0
    o_ref[...] = jnp.where(far_ref[:, :rank] == s, part, kept)


def half_kernel(i, x_ref, m_ref, *rest):
    o_ref = rest[-1]
    k_half = x_ref.shape[1] // 2
    part = lax.dot_general(
        x_ref[:, i * k_half : (i + 1) * k_half],
        m_ref[:, :k_half],
        (((1,), (1,)), ((), ())),
        preferred_element_type=jnp.float32,
    )
    o_ref[...] = part + rest[0][...] if len(rest) > 1 else part


def lift(steps, far_ref, total, ups):
    high = total.astype(jnp.bfloat16)
    low = (total - high.astype(jnp.float32)).astype(jnp.bfloat16)
    rank = total.shape[1]
    far = far_ref[:, :rank]
    b_all = jnp.concatenate(ups, axis=0)
    out = None
    for part in (low, high):
        part = part.astype(jnp.float32)
        wide = jnp.concatenate([jnp.where(far == s, part, 0.0).astype(jnp.bfloat16) for s in steps], axis=1)
        product = jnp.dot(wide, b_all, preferred_element_type=jnp.float32)
        out = product if out is None else out + product
    return out


def up_kernel(steps, far_ref, own_ref, other_ref, here_ref, there_ref, *rest):
    o_ref = rest[-1]
    rank = own_ref.shape[1]
    b_half = o_ref.shape[1] // 2
    ups = []
    for m_ref in rest[:-1]:
        last = m_ref.shape[1]
        ups.append(jnp.concatenate([m_ref[:rank, last - b_half :], m_ref[rank:, last - b_half :]], axis=1))
    lifted = lift(steps, far_ref, own_ref[...] + other_ref[...], ups)
    o_ref[...] = here_ref[...] + there_ref[...] + lifted


def last_kernel(s, far_ref, own_ref, other_ref, base_ref, p_ref, q_ref, o_ref):
    first = p_ref.shape[1] - o_ref.shape[1] // 2
    ups = [jnp.concatenate([p_ref[:, first:], q_ref[:, first:]], axis=1)]
    lifted = lift([s], far_ref, own_ref[...] + other_ref[...], ups)
    o_ref[...] = (base_ref[...] + lifted).astype(jnp.bfloat16)


def shards(n, requests, adapter_index, storage_slot_index, key_base_weight, down_factor, up_factor):
    rows, half = requests.shape
    rank = down_factor.shape[2]
    keys = up_factor.shape[2]
    out_keys = keys // 2
    f32 = jnp.float32

    order = ring_of(n)
    forth, back = [], []
    for j in range(n):
        a, b = order[j], order[(j + 1) % n]
        forth += [(2 * a, 2 * b), (2 * b + 1, 2 * a + 1)]
        back += [(2 * b, 2 * a), (2 * a + 1, 2 * b + 1)]
    swap = [(0, 1), (1, 0)]
    both = ("dp", "tensor")

    own = call(
        pack_kernel,
        [((2 * rank, half // 2 + out_keys // 2), jnp.bfloat16)],
        [HBM, HBM],
        down_factor[0].T,
        up_factor[0],
        mib=16,
        scratch=[pltpu.SemaphoreType.DMA((4,))],
    )
    p = own
    opposite = n % 2 == 0 and n > 1
    rounds = (n - 1) // 2

    x, there, here = call(
        base_kernel,
        [((rows, half), jnp.bfloat16), ((rows, out_keys), f32), ((rows, out_keys), f32)],
        [HBM, HBM],
        *tie((own, requests, key_base_weight))[1:],
        mib=50,
        scratch=[
            pltpu.VMEM((half, keys), jnp.bfloat16),
            pltpu.SemaphoreType.DMA((BASE_STEPS,)),
            pltpu.SemaphoreType.DMA((BASE_STEPS,)),
        ],
    )
    there, q = tie((there, own))
    from_there = lax.ppermute(there, "tensor", swap)

    def far_of(index):
        kernel = functools.partial(far_kernel, n)
        return call(kernel, [((rows, LANES), jnp.int32)], [VMEM, SMEM], index, storage_slot_index)

    def down_of(message, s, *total, moved=1000):
        return call(
            functools.partial(down_kernel, s),
            [((rows, rank), f32)],
            [VMEM] * (3 + len(total)),
            tie((message, x))[1],
            message,
            far,
            *total,
            moved=moved,
        )

    total = None
    pieces = [(0, own)]
    for s in range(1, rounds + 1):
        p = lax.ppermute(p, both, forth)
        q = lax.ppermute(q, both, back)
        if s == 1:
            index = tie((p, adapter_index))[1]
            far = far_of(index)
            total = down_of(own, 0)
        else:
            total = down_of(pieces[-1][1], pieces[-1][0], total)
            total, p = tie((total, p))
        pieces.append((s, p))
        total = down_of(p, s, total)
        if s == min(2, rounds):
            from_there, q = tie((from_there, q))
        total, q = tie((total, q))
        pieces.append((n - s, q))
    if total is None:
        far = far_of(adapter_index)
        total = down_of(own, 0)
    else:
        total = down_of(pieces[-1][1], pieces[-1][0], total)

    if opposite:
        p = lax.ppermute(p[:rank], both, forth)
        q = lax.ppermute(q[rank:], both, back)
    other = lax.ppermute(total, "tensor", swap)
    messages = [m if n <= 16 else m[:, half // 2 :] for _, m in pieces]
    base = call(
        functools.partial(up_kernel, [s for s, _ in pieces]),
        [((rows, out_keys), f32)],
        [VMEM] * (5 + len(messages)),
        far,
        total,
        other,
        here,
        from_there,
        *messages,
        mib=32 if n > 16 else 16,
    )
    if not opposite:
        return base.astype(jnp.bfloat16)
    base, p = tie((base, p))
    total = call(functools.partial(half_kernel, 0), [((rows, rank), f32)], [VMEM] * 2, x, p)
    total, q = tie((total, q))
    total = call(functools.partial(half_kernel, 1), [((rows, rank), f32)], [VMEM] * 3, x, q, total)
    other = lax.ppermute(total, "tensor", swap)
    return call(
        functools.partial(last_kernel, n // 2),
        [((rows, out_keys), jnp.bfloat16)],
        [VMEM] * 6,
        far,
        total,
        other,
        base,
        p,
        q,
    )


def solution(mesh):
    placed = (
        P(("groups", "dp"), "tensor"),
        P(("groups", "dp"), None),
        P("groups"),
        P("tensor", None),
        P(("groups", "dp"), "tensor", None),
        P(("groups", "dp"), None, None),
    )
    n = mesh.shape["dp"]
    return jax.shard_map(
        functools.partial(shards, n),
        mesh=mesh,
        in_specs=placed,
        out_specs=P(("groups", "dp"), "tensor"),
        check_vma=False,
    )
```

```python
import functools

import jax
import jax.numpy as jnp
from jax import lax
from jax.experimental import pallas as pl
from jax.experimental.pallas import tpu as pltpu
from jax.sharding import PartitionSpec as P

LANES = 128
BASE_STEPS = 8
tie = lax.optimization_barrier
VMEM = pl.BlockSpec(memory_space=pltpu.VMEM)
SMEM = pl.BlockSpec(memory_space=pltpu.SMEM)
HBM = pl.BlockSpec(memory_space=pl.ANY)


def snakes(n):
    return n % 2 == 0 and n <= 16


def ring_of(n):
    if snakes(n):
        return list(range(0, n, 2)) + list(range(n - 1, 0, -2))
    return list(range(n))


def place_in(n, i):
    return jnp.where(i % 2 == 0, i // 2, n - 1 - i // 2) if snakes(n) else i


def call(kernel, outs, in_specs, *args, mib=16, scratch=(), moved=1000):
    shapes = [jax.ShapeDtypeStruct(shape, dtype) for shape, dtype in outs]
    got = pl.pallas_call(
        kernel,
        in_specs=in_specs,
        out_specs=[VMEM] * len(outs),
        out_shape=shapes,
        scratch_shapes=scratch,
        compiler_params=pltpu.CompilerParams(vmem_limit_bytes=mib << 20),
        cost_estimate=pl.CostEstimate(flops=1000, bytes_accessed=moved, transcendentals=0),
    )(*args)
    return got[0] if len(outs) == 1 else got


def pack_kernel(a_ref, b_ref, o_ref, sems):
    rank, half = a_ref.shape
    k_half, b_half = half // 2, o_ref.shape[1] - half // 2
    first = lax.axis_index("tensor") * (2 * b_half)
    copies = []
    for i in range(2):
        rows = pl.ds(i * rank, rank)
        b_first = pl.multiple_of(first + i * b_half, b_half)
        copies += [
            (a_ref.at[:, pl.ds(i * k_half, k_half)], o_ref.at[rows, pl.ds(0, k_half)]),
            (b_ref.at[:, pl.ds(b_first, b_half)], o_ref.at[rows, pl.ds(k_half, b_half)]),
        ]
    copies = [pltpu.make_async_copy(*c, sems.at[i]) for i, c in enumerate(copies)]
    for c in copies:
        c.start()
    for c in copies:
        c.wait()


def far_kernel(n, index_ref, storage_ref, o_ref):
    here = place_in(n, lax.axis_index("dp"))
    way = 1 - 2 * lax.axis_index("tensor")
    index = index_ref[...]

    def look(j, far):
        return jnp.where(index == j, lax.rem((here - place_in(n, storage_ref[j])) * way + n, n), far)

    far = lax.fori_loop(0, n, look, jnp.zeros_like(index))
    o_ref[...] = jnp.broadcast_to(far, o_ref.shape)


def base_kernel(x_hbm, w_hbm, x_ref, there_ref, here_ref, w_ref, x_sems, w_sems):
    depth = x_hbm.shape[1] // BASE_STEPS
    keys = here_ref.shape[1]
    core = lax.axis_index("tensor")
    copies = []
    for i in range(BASE_STEPS):
        k = pl.ds(i * depth, depth)
        copies.append(
            (
                pltpu.make_async_copy(x_hbm.at[:, k], x_ref.at[:, k], x_sems.at[i]),
                pltpu.make_async_copy(w_hbm.at[k, :], w_ref.at[k, :], w_sems.at[i]),
            )
        )
        for c in copies[-1]:
            c.start()
    for i in range(BASE_STEPS):
        k = pl.ds(i * depth, depth)
        for c in copies[i]:
            c.wait()
        for o_ref, side in ((there_ref, 1 - core), (here_ref, core)):
            columns = pl.ds(pl.multiple_of(side * keys, keys), keys)
            product = jnp.dot(x_ref[:, k], w_ref[k, columns], preferred_element_type=jnp.float32)
            o_ref[...] = product if i == 0 else o_ref[...] + product


def down_kernel(s, x_ref, m_ref, far_ref, *rest):
    o_ref = rest[-1]
    rank = o_ref.shape[1]
    k_half = x_ref.shape[1] // 2
    part = None
    for i in range(2):
        product = lax.dot_general(
            x_ref[:, i * k_half : (i + 1) * k_half],
            m_ref[i * rank : (i + 1) * rank, :k_half],
            (((1,), (1,)), ((), ())),
            preferred_element_type=jnp.float32,
        )
        part = product if part is None else part + product
    kept = rest[0][...] if len(rest) > 1 else 0.0
    o_ref[...] = jnp.where(far_ref[:, :rank] == s, part, kept)


def half_kernel(i, x_ref, m_ref, *rest):
    o_ref = rest[-1]
    k_half = x_ref.shape[1] // 2
    part = lax.dot_general(
        x_ref[:, i * k_half : (i + 1) * k_half],
        m_ref[:, :k_half],
        (((1,), (1,)), ((), ())),
        preferred_element_type=jnp.float32,
    )
    o_ref[...] = part + rest[0][...] if len(rest) > 1 else part


def lift(steps, far_ref, total, ups):
    high = total.astype(jnp.bfloat16)
    low = (total - high.astype(jnp.float32)).astype(jnp.bfloat16)
    rank = total.shape[1]
    far = far_ref[:, :rank]
    b_all = jnp.concatenate(ups, axis=0)
    out = None
    for part in (low, high):
        part = part.astype(jnp.float32)
        wide = jnp.concatenate([jnp.where(far == s, part, 0.0).astype(jnp.bfloat16) for s in steps], axis=1)
        product = jnp.dot(wide, b_all, preferred_element_type=jnp.float32)
        out = product if out is None else out + product
    return out


def up_kernel(steps, far_ref, own_ref, other_ref, here_ref, there_ref, *rest):
    o_ref = rest[-1]
    rank = own_ref.shape[1]
    b_half = o_ref.shape[1] // 2
    ups = []
    for m_ref in rest[:-1]:
        last = m_ref.shape[1]
        ups.append(jnp.concatenate([m_ref[:rank, last - b_half :], m_ref[rank:, last - b_half :]], axis=1))
    lifted = lift(steps, far_ref, own_ref[...] + other_ref[...], ups)
    o_ref[...] = here_ref[...] + there_ref[...] + lifted


def last_kernel(s, far_ref, own_ref, other_ref, base_ref, p_ref, q_ref, o_ref):
    first = p_ref.shape[1] - o_ref.shape[1] // 2
    ups = [jnp.concatenate([p_ref[:, first:], q_ref[:, first:]], axis=1)]
    lifted = lift([s], far_ref, own_ref[...] + other_ref[...], ups)
    o_ref[...] = (base_ref[...] + lifted).astype(jnp.bfloat16)


def shards(n, requests, adapter_index, storage_slot_index, key_base_weight, down_factor, up_factor):
    rows, half = requests.shape
    rank = down_factor.shape[2]
    keys = up_factor.shape[2]
    out_keys = keys // 2
    f32 = jnp.float32

    order = ring_of(n)
    forth, back = [], []
    for j in range(n):
        a, b = order[j], order[(j + 1) % n]
        forth += [(2 * a, 2 * b), (2 * b + 1, 2 * a + 1)]
        back += [(2 * b, 2 * a), (2 * a + 1, 2 * b + 1)]
    swap = [(0, 1), (1, 0)]
    both = ("dp", "tensor")

    own = call(
        pack_kernel,
        [((2 * rank, half // 2 + out_keys // 2), jnp.bfloat16)],
        [HBM, HBM],
        down_factor[0].T,
        up_factor[0],
        mib=16,
        scratch=[pltpu.SemaphoreType.DMA((4,))],
    )
    p = own
    opposite = n % 2 == 0 and n > 1
    rounds = (n - 1) // 2

    x, there, here = call(
        base_kernel,
        [((rows, half), jnp.bfloat16), ((rows, out_keys), f32), ((rows, out_keys), f32)],
        [HBM, HBM],
        *tie((own, requests, key_base_weight))[1:],
        mib=50,
        scratch=[
            pltpu.VMEM((half, keys), jnp.bfloat16),
            pltpu.SemaphoreType.DMA((BASE_STEPS,)),
            pltpu.SemaphoreType.DMA((BASE_STEPS,)),
        ],
    )
    there, q = tie((there, own))
    from_there = lax.ppermute(there, "tensor", swap)

    def far_of(index):
        kernel = functools.partial(far_kernel, n)
        return call(kernel, [((rows, LANES), jnp.int32)], [VMEM, SMEM], index, storage_slot_index)

    def down_of(message, s, *total, moved=1000):
        return call(
            functools.partial(down_kernel, s),
            [((rows, rank), f32)],
            [VMEM] * (3 + len(total)),
            tie((message, x))[1],
            message,
            far,
            *total,
            moved=moved,
        )

    total = None
    pieces = [(0, own)]
    for s in range(1, rounds + 1):
        p = lax.ppermute(p, both, forth)
        q = lax.ppermute(q, both, back)
        if s == 1:
            far = far_of(tie((there, adapter_index))[1])
            total = down_of(own, 0)
            total, p = tie((total, p))
        else:
            total = down_of(pieces[-1][1], pieces[-1][0], total)
            total, p = tie((total, p))
        pieces.append((s, p))
        total = down_of(p, s, total)
        if s == min(2, rounds):
            from_there, q = tie((from_there, q))
        total, q = tie((total, q))
        pieces.append((n - s, q))
    if total is None:
        far = far_of(adapter_index)
        total = down_of(own, 0)
    else:
        total = down_of(pieces[-1][1], pieces[-1][0], total)

    if opposite:
        p = lax.ppermute(p[:rank], both, forth)
        q = lax.ppermute(q[rank:], both, back)
    other = lax.ppermute(total, "tensor", swap)
    messages = [m if n <= 16 else m[:, half // 2 :] for _, m in pieces]
    base = call(
        functools.partial(up_kernel, [s for s, _ in pieces]),
        [((rows, out_keys), f32)],
        [VMEM] * (5 + len(messages)),
        far,
        total,
        other,
        here,
        from_there,
        *messages,
        mib=32 if n > 16 else 16,
    )
    if not opposite:
        return base.astype(jnp.bfloat16)
    base, p = tie((base, p))
    total = call(functools.partial(half_kernel, 0), [((rows, rank), f32)], [VMEM] * 2, x, p)
    total, q = tie((total, q))
    total = call(functools.partial(half_kernel, 1), [((rows, rank), f32)], [VMEM] * 3, x, q, total)
    other = lax.ppermute(total, "tensor", swap)
    return call(
        functools.partial(last_kernel, n // 2),
        [((rows, out_keys), jnp.bfloat16)],
        [VMEM] * 6,
        far,
        total,
        other,
        base,
        p,
        q,
    )


def solution(mesh):
    placed = (
        P(("groups", "dp"), "tensor"),
        P(("groups", "dp"), None),
        P("groups"),
        P("tensor", None),
        P(("groups", "dp"), "tensor", None),
        P(("groups", "dp"), None, None),
    )
    n = mesh.shape["dp"]
    return jax.shard_map(
        functools.partial(shards, n),
        mesh=mesh,
        in_specs=placed,
        out_specs=P(("groups", "dp"), "tensor"),
        check_vma=False,
    )
```

```python
import functools

import jax
import jax.numpy as jnp
from jax import lax
from jax.experimental import pallas as pl
from jax.experimental.pallas import tpu as pltpu
from jax.sharding import PartitionSpec as P

LANES = 128
BASE_STEPS = 8
BASE_MIB = 48
PACK_MIB = 60
tie = lax.optimization_barrier
VMEM = pl.BlockSpec(memory_space=pltpu.VMEM)
SMEM = pl.BlockSpec(memory_space=pltpu.SMEM)
HBM = pl.BlockSpec(memory_space=pl.ANY)


def snakes(n):
    return n % 2 == 0 and n <= 16


def ring_of(n):
    if snakes(n):
        return list(range(0, n, 2)) + list(range(n - 1, 0, -2))
    return list(range(n))


def place_in(n, i):
    return jnp.where(i % 2 == 0, i // 2, n - 1 - i // 2) if snakes(n) else i


def call(kernel, outs, in_specs, *args, mib=16, scratch=(), moved=1000, out_space=VMEM):
    shapes = [jax.ShapeDtypeStruct(shape, dtype) for shape, dtype in outs]
    got = pl.pallas_call(
        kernel,
        in_specs=in_specs,
        out_specs=[out_space] * len(outs),
        out_shape=shapes,
        scratch_shapes=scratch,
        compiler_params=pltpu.CompilerParams(vmem_limit_bytes=mib << 20),
        cost_estimate=pl.CostEstimate(flops=1000, bytes_accessed=moved, transcendentals=0),
    )(*args)
    return got[0] if len(outs) == 1 else got


def pack_kernel(a_ref, b_ref, o_ref, sems):
    rank, half = a_ref.shape
    k_half, b_half = half // 2, o_ref.shape[1] - half // 2
    first = lax.axis_index("tensor") * (2 * b_half)
    copies = []
    for i in range(2):
        rows = pl.ds(i * rank, rank)
        b_first = pl.multiple_of(first + i * b_half, b_half)
        copies += [
            (a_ref.at[:, pl.ds(i * k_half, k_half)], o_ref.at[rows, pl.ds(0, k_half)]),
            (b_ref.at[:, pl.ds(b_first, b_half)], o_ref.at[rows, pl.ds(k_half, b_half)]),
        ]
    copies = [pltpu.make_async_copy(*c, sems.at[i]) for i, c in enumerate(copies)]
    for c in copies:
        c.start()
    for c in copies:
        c.wait()


def far_kernel(n, index_ref, storage_ref, o_ref):
    here = place_in(n, lax.axis_index("dp"))
    way = 1 - 2 * lax.axis_index("tensor")
    index = index_ref[...]

    def look(j, far):
        return jnp.where(index == j, lax.rem((here - place_in(n, storage_ref[j])) * way + n, n), far)

    far = lax.fori_loop(0, n, look, jnp.zeros_like(index))
    o_ref[...] = jnp.broadcast_to(far, o_ref.shape)


def base_kernel(x_hbm, w_hbm, x_ref, o_ref, w_ref, x_sems, w_sems):
    depth = x_hbm.shape[1] // BASE_STEPS
    keys = o_ref.shape[1]
    columns = pl.ds(pl.multiple_of((1 - lax.axis_index("tensor")) * keys, keys), keys)
    copies = []
    for i in range(BASE_STEPS):
        k = pl.ds(i * depth, depth)
        copies.append(
            (
                pltpu.make_async_copy(x_hbm.at[:, k], x_ref.at[:, k], x_sems.at[i]),
                pltpu.make_async_copy(w_hbm.at[k, columns], w_ref.at[k, :], w_sems.at[i]),
            )
        )
        for c in copies[-1]:
            c.start()
    for i in range(BASE_STEPS):
        k = pl.ds(i * depth, depth)
        for c in copies[i]:
            c.wait()
        product = jnp.dot(x_ref[:, k], w_ref[k, :], preferred_element_type=jnp.float32)
        o_ref[...] = product if i == 0 else o_ref[...] + product


def here_kernel(x_ref, w_hbm, o_ref, w_ref, w_sems):
    depth = x_ref.shape[1] // BASE_STEPS
    keys = o_ref.shape[1]
    columns = pl.ds(pl.multiple_of(lax.axis_index("tensor") * keys, keys), keys)
    copies = []
    for i in range(BASE_STEPS):
        k = pl.ds(i * depth, depth)
        copies.append(pltpu.make_async_copy(w_hbm.at[k, columns], w_ref.at[k, :], w_sems.at[i]))
        copies[-1].start()
    for i in range(BASE_STEPS):
        k = pl.ds(i * depth, depth)
        copies[i].wait()
        product = jnp.dot(x_ref[:, k], w_ref[k, :], preferred_element_type=jnp.float32)
        o_ref[...] = product if i == 0 else o_ref[...] + product


def halves_of(m_refs, rank):
    if len(m_refs) == 2:
        return m_refs
    return [m_refs[0].at[pl.ds(i * rank, rank), :] for i in range(2)]


def down_kernel(s, split, x_ref, far_ref, *rest):
    o_ref = rest[-1]
    rank = o_ref.shape[1]
    k_half = x_ref.shape[1] // 2
    m_refs = rest[: 1 + split]
    rest = rest[1 + split :]
    part = None
    for i, m_ref in enumerate(halves_of(m_refs, rank)):
        product = lax.dot_general(
            x_ref[:, i * k_half : (i + 1) * k_half],
            m_ref[:, :k_half],
            (((1,), (1,)), ((), ())),
            preferred_element_type=jnp.float32,
        )
        part = product if part is None else part + product
    kept = rest[0][...] if len(rest) > 1 else 0.0
    o_ref[...] = jnp.where(far_ref[:, :rank] == s, part, kept)


def half_kernel(i, x_ref, m_ref, *rest):
    o_ref = rest[-1]
    k_half = x_ref.shape[1] // 2
    part = lax.dot_general(
        x_ref[:, i * k_half : (i + 1) * k_half],
        m_ref[:, :k_half],
        (((1,), (1,)), ((), ())),
        preferred_element_type=jnp.float32,
    )
    o_ref[...] = part + rest[0][...] if len(rest) > 1 else part


def lift(steps, far_ref, total, ups):
    high = total.astype(jnp.bfloat16)
    low = (total - high.astype(jnp.float32)).astype(jnp.bfloat16)
    rank = total.shape[1]
    far = far_ref[:, :rank]
    b_all = jnp.concatenate(ups, axis=0)
    out = None
    for part in (low, high):
        part = part.astype(jnp.float32)
        wide = jnp.concatenate([jnp.where(far == s, part, 0.0).astype(jnp.bfloat16) for s in steps], axis=1)
        product = jnp.dot(wide, b_all, preferred_element_type=jnp.float32)
        out = product if out is None else out + product
    return out


def up_kernel(steps, counts, far_ref, own_ref, other_ref, here_ref, there_ref, *rest):
    o_ref = rest[-1]
    rank = own_ref.shape[1]
    b_half = o_ref.shape[1] // 2
    ups = []
    for count in counts:
        parts = halves_of(rest[:count], rank)
        rest = rest[count:]
        ups.append(jnp.concatenate([m[:, m.shape[1] - b_half :] for m in parts], axis=1))
    lifted = lift(steps, far_ref, own_ref[...] + other_ref[...], ups)
    o_ref[...] = here_ref[...] + there_ref[...] + lifted


def last_kernel(s, far_ref, own_ref, other_ref, base_ref, p_ref, q_ref, o_ref):
    first = p_ref.shape[1] - o_ref.shape[1] // 2
    ups = [jnp.concatenate([p_ref[:, first:], q_ref[:, first:]], axis=1)]
    lifted = lift([s], far_ref, own_ref[...] + other_ref[...], ups)
    o_ref[...] = (base_ref[...] + lifted).astype(jnp.bfloat16)


def shards(n, requests, adapter_index, storage_slot_index, key_base_weight, down_factor, up_factor):
    rows, half = requests.shape
    rank = down_factor.shape[2]
    keys = up_factor.shape[2]
    out_keys = keys // 2
    f32 = jnp.float32

    order = ring_of(n)
    forth, back = [], []
    for j in range(n):
        a, b = order[j], order[(j + 1) % n]
        forth += [(2 * a, 2 * b), (2 * b + 1, 2 * a + 1)]
        back += [(2 * b, 2 * a), (2 * a + 1, 2 * b + 1)]
    swap = [(0, 1), (1, 0)]
    both = ("dp", "tensor")

    own = call(
        pack_kernel,
        [((2 * rank, half // 2 + out_keys // 2), jnp.bfloat16)],
        [HBM, HBM],
        down_factor[0].T,
        up_factor[0],
        mib=PACK_MIB,
        scratch=[pltpu.SemaphoreType.DMA((4,))],
    )
    p = own
    opposite = n % 2 == 0 and n > 1
    rounds = (n - 1) // 2

    _, x_hbm, w_hbm = tie((own, requests, key_base_weight))
    x, there = call(
        base_kernel,
        [((rows, half), jnp.bfloat16), ((rows, out_keys), f32)],
        [HBM, HBM],
        x_hbm,
        w_hbm,
        mib=BASE_MIB,
        scratch=[
            pltpu.VMEM((half, out_keys), jnp.bfloat16),
            pltpu.SemaphoreType.DMA((BASE_STEPS,)),
            pltpu.SemaphoreType.DMA((BASE_STEPS,)),
        ],
    )
    there, q = tie((there, own))
    from_there = lax.ppermute(there, "tensor", swap)
    here = call(
        here_kernel,
        [((rows, out_keys), f32)],
        [VMEM, HBM],
        tie((there, x))[1],
        key_base_weight,
        mib=BASE_MIB,
        scratch=[pltpu.VMEM((half, out_keys), jnp.bfloat16), pltpu.SemaphoreType.DMA((BASE_STEPS,))],
    )

    def far_of(index):
        kernel = functools.partial(far_kernel, n)
        return call(kernel, [((rows, LANES), jnp.int32)], [VMEM, SMEM], index, storage_slot_index)

    def down_of(message, s, *total):
        return call(
            functools.partial(down_kernel, s, len(message) - 1),
            [((rows, rank), f32)],
            [VMEM] * (2 + len(message) + len(total)),
            tie((*message, x))[-1],
            far,
            *message,
            *total,
        )

    total = None
    pieces = [(0, (own,))]
    for s in range(1, rounds + 1):
        halved = False
        if halved:
            p = tuple(lax.ppermute(h, both, forth) for h in (p[:rank], p[rank:]))
            q = tuple(lax.ppermute(h, both, back) for h in (q[rank:], q[:rank]))[::-1]
        else:
            p = (lax.ppermute(p, both, forth),)
            q = (lax.ppermute(q, both, back),)
        if s == 1:
            far = far_of(tie((there, adapter_index))[1])
            here, far, *p = tie((here, far, *p))
            total = down_of((own,), 0)
        else:
            total = down_of(pieces[-1][1], pieces[-1][0], total)
            total, *p = tie((total, *p))
        pieces.append((s, tuple(p)))
        if halved:
            pieces.append((n - s, tuple(q)))
            break
        total = down_of(pieces[-1][1], s, total)
        if s == min(2, rounds):
            from_there, *q = tie((from_there, *q))
        total, *q = tie((total, *q))
        pieces.append((n - s, tuple(q)))
        p, q = p[0], q[0]
    if opposite:
        p, q = tie((p, q)) if rounds else (p, q)
        p, q = p[:rank], q[rank:]
        p = lax.ppermute(p, both, forth)
        q = lax.ppermute(q, both, back)
    if total is None:
        far = far_of(adapter_index)
        total = down_of((own,), 0)
    else:
        total = down_of(pieces[-1][1], pieces[-1][0], total)
    other = lax.ppermute(total, "tensor", swap)
    messages = [m if n <= 16 else m[:, half // 2 :] for _, ms in pieces for m in ms]
    base = call(
        functools.partial(up_kernel, [s for s, _ in pieces], [len(ms) for _, ms in pieces]),
        [((rows, out_keys), f32)],
        [VMEM] * (5 + len(messages)),
        far,
        total,
        other,
        here,
        from_there,
        *messages,
        mib=32 if n > 16 else 16,
    )
    if not opposite:
        return base.astype(jnp.bfloat16)
    base, p = tie((base, p))
    total = call(functools.partial(half_kernel, 0), [((rows, rank), f32)], [VMEM] * 2, x, p)
    total, q = tie((total, q))
    total = call(functools.partial(half_kernel, 1), [((rows, rank), f32)], [VMEM] * 3, x, q, total)
    other = lax.ppermute(total, "tensor", swap)
    return call(
        functools.partial(last_kernel, n // 2),
        [((rows, out_keys), jnp.bfloat16)],
        [VMEM] * 6,
        far,
        total,
        other,
        base,
        p,
        q,
    )


def solution(mesh):
    placed = (
        P(("groups", "dp"), "tensor"),
        P(("groups", "dp"), None),
        P("groups"),
        P("tensor", None),
        P(("groups", "dp"), "tensor", None),
        P(("groups", "dp"), None, None),
    )
    n = mesh.shape["dp"]
    return jax.shard_map(
        functools.partial(shards, n),
        mesh=mesh,
        in_specs=placed,
        out_specs=P(("groups", "dp"), "tensor"),
        check_vma=False,
    )
```

```python
import functools

import jax
import jax.numpy as jnp
from jax import lax
from jax.experimental import pallas as pl
from jax.experimental.pallas import tpu as pltpu
from jax.sharding import PartitionSpec as P

LANES = 128
BASE_STEPS = 8
BASE_MIB = 48
PACK_MIB = 60
tie = lax.optimization_barrier
VMEM = pl.BlockSpec(memory_space=pltpu.VMEM)
SMEM = pl.BlockSpec(memory_space=pltpu.SMEM)
HBM = pl.BlockSpec(memory_space=pl.ANY)


def snakes(n):
    return n % 2 == 0 and n <= 16


def ring_of(n):
    if snakes(n):
        return list(range(0, n, 2)) + list(range(n - 1, 0, -2))
    return list(range(n))


def place_in(n, i):
    return jnp.where(i % 2 == 0, i // 2, n - 1 - i // 2) if snakes(n) else i


def call(kernel, outs, in_specs, *args, mib=16, scratch=(), moved=1000, out_space=VMEM):
    shapes = [jax.ShapeDtypeStruct(shape, dtype) for shape, dtype in outs]
    got = pl.pallas_call(
        kernel,
        in_specs=in_specs,
        out_specs=[out_space] * len(outs),
        out_shape=shapes,
        scratch_shapes=scratch,
        compiler_params=pltpu.CompilerParams(vmem_limit_bytes=mib << 20),
        cost_estimate=pl.CostEstimate(flops=1000, bytes_accessed=moved, transcendentals=0),
    )(*args)
    return got[0] if len(outs) == 1 else got


def pack_kernel(a_ref, b_ref, o_ref, sems):
    rank, half = a_ref.shape
    k_half, b_half = half // 2, o_ref.shape[1] - half // 2
    first = lax.axis_index("tensor") * (2 * b_half)
    copies = []
    for i in range(2):
        rows = pl.ds(i * rank, rank)
        b_first = pl.multiple_of(first + i * b_half, b_half)
        copies += [
            (a_ref.at[:, pl.ds(i * k_half, k_half)], o_ref.at[rows, pl.ds(0, k_half)]),
            (b_ref.at[:, pl.ds(b_first, b_half)], o_ref.at[rows, pl.ds(k_half, b_half)]),
        ]
    copies = [pltpu.make_async_copy(*c, sems.at[i]) for i, c in enumerate(copies)]
    for c in copies:
        c.start()
    for c in copies:
        c.wait()


def far_kernel(n, index_ref, storage_ref, o_ref):
    here = place_in(n, lax.axis_index("dp"))
    way = 1 - 2 * lax.axis_index("tensor")
    index = index_ref[...]

    def look(j, far):
        return jnp.where(index == j, lax.rem((here - place_in(n, storage_ref[j])) * way + n, n), far)

    far = lax.fori_loop(0, n, look, jnp.zeros_like(index))
    o_ref[...] = jnp.broadcast_to(far, o_ref.shape)


def base_kernel(x_hbm, w_hbm, x_ref, o_ref, w_ref, x_sems, w_sems):
    depth = x_hbm.shape[1] // BASE_STEPS
    keys = o_ref.shape[1]
    columns = pl.ds(pl.multiple_of((1 - lax.axis_index("tensor")) * keys, keys), keys)
    copies = []
    for i in range(BASE_STEPS):
        k = pl.ds(i * depth, depth)
        copies.append(
            (
                pltpu.make_async_copy(x_hbm.at[:, k], x_ref.at[:, k], x_sems.at[i]),
                pltpu.make_async_copy(w_hbm.at[k, columns], w_ref.at[k, :], w_sems.at[i]),
            )
        )
        for c in copies[-1]:
            c.start()
    for i in range(BASE_STEPS):
        k = pl.ds(i * depth, depth)
        for c in copies[i]:
            c.wait()
        product = jnp.dot(x_ref[:, k], w_ref[k, :], preferred_element_type=jnp.float32)
        o_ref[...] = product if i == 0 else o_ref[...] + product


def here_kernel(x_ref, w_hbm, o_ref, w_ref, w_sems):
    depth = x_ref.shape[1] // BASE_STEPS
    keys = o_ref.shape[1]
    columns = pl.ds(pl.multiple_of(lax.axis_index("tensor") * keys, keys), keys)
    copies = []
    for i in range(BASE_STEPS):
        k = pl.ds(i * depth, depth)
        copies.append(pltpu.make_async_copy(w_hbm.at[k, columns], w_ref.at[k, :], w_sems.at[i]))
        copies[-1].start()
    for i in range(BASE_STEPS):
        k = pl.ds(i * depth, depth)
        copies[i].wait()
        product = jnp.dot(x_ref[:, k], w_ref[k, :], preferred_element_type=jnp.float32)
        o_ref[...] = product if i == 0 else o_ref[...] + product


def halves_of(m_refs, rank):
    if len(m_refs) == 2:
        return m_refs
    return [m_refs[0].at[pl.ds(i * rank, rank), :] for i in range(2)]


def down_kernel(s, split, x_ref, far_ref, *rest):
    o_ref = rest[-1]
    rank = o_ref.shape[1]
    k_half = x_ref.shape[1] // 2
    m_refs = rest[: 1 + split]
    rest = rest[1 + split :]
    part = None
    for i, m_ref in enumerate(halves_of(m_refs, rank)):
        product = lax.dot_general(
            x_ref[:, i * k_half : (i + 1) * k_half],
            m_ref[:, :k_half],
            (((1,), (1,)), ((), ())),
            preferred_element_type=jnp.float32,
        )
        part = product if part is None else part + product
    kept = rest[0][...] if len(rest) > 1 else 0.0
    o_ref[...] = jnp.where(far_ref[:, :rank] == s, part, kept)


def half_kernel(i, s, x_ref, far_ref, m_ref, *rest):
    o_ref = rest[-1]
    k_half = x_ref.shape[1] // 2
    part = lax.dot_general(
        x_ref[:, i * k_half : (i + 1) * k_half],
        m_ref[:, :k_half],
        (((1,), (1,)), ((), ())),
        preferred_element_type=jnp.float32,
    )
    if i == 1:
        kept = rest[1][...] if len(rest) > 2 else 0.0
        part = jnp.where(far_ref[:, : part.shape[1]] == s, part + rest[0][...], kept)
    o_ref[...] = part


def lift(steps, far_ref, total, ups):
    high = total.astype(jnp.bfloat16)
    low = (total - high.astype(jnp.float32)).astype(jnp.bfloat16)
    rank = total.shape[1]
    far = far_ref[:, :rank]
    b_all = jnp.concatenate(ups, axis=0)
    out = None
    for part in (low, high):
        part = part.astype(jnp.float32)
        wide = jnp.concatenate([jnp.where(far == s, part, 0.0).astype(jnp.bfloat16) for s in steps], axis=1)
        product = jnp.dot(wide, b_all, preferred_element_type=jnp.float32)
        out = product if out is None else out + product
    return out


def ups_of(counts, refs, rank, keys):
    ups = []
    for count in counts:
        parts = halves_of(refs[:count], rank)
        refs = refs[count:]
        ups.append(jnp.concatenate([m[:, m.shape[1] - keys // 2 :] for m in parts], axis=1))
    return ups


def up_kernel(steps, counts, far_ref, own_ref, other_ref, here_ref, there_ref, *rest):
    o_ref = rest[-1]
    ups = ups_of(counts, rest[:-1], own_ref.shape[1], o_ref.shape[1])
    lifted = lift(steps, far_ref, own_ref[...] + other_ref[...], ups)
    o_ref[...] = here_ref[...] + there_ref[...] + lifted


def last_kernel(steps, counts, far_ref, own_ref, other_ref, base_ref, *rest):
    o_ref = rest[-1]
    ups = ups_of(counts, rest[:-1], own_ref.shape[1], o_ref.shape[1])
    lifted = lift(steps, far_ref, own_ref[...] + other_ref[...], ups)
    o_ref[...] = (base_ref[...] + lifted).astype(jnp.bfloat16)


def shards(n, requests, adapter_index, storage_slot_index, key_base_weight, down_factor, up_factor):
    rows, half = requests.shape
    rank = down_factor.shape[2]
    keys = up_factor.shape[2]
    out_keys = keys // 2
    f32 = jnp.float32

    order = ring_of(n)
    forth, back = [], []
    for j in range(n):
        a, b = order[j], order[(j + 1) % n]
        forth += [(2 * a, 2 * b), (2 * b + 1, 2 * a + 1)]
        back += [(2 * b, 2 * a), (2 * a + 1, 2 * b + 1)]
    swap = [(0, 1), (1, 0)]
    both = ("dp", "tensor")

    own = call(
        pack_kernel,
        [((2 * rank, half // 2 + out_keys // 2), jnp.bfloat16)],
        [HBM, HBM],
        down_factor[0].T,
        up_factor[0],
        mib=PACK_MIB,
        scratch=[pltpu.SemaphoreType.DMA((4,))],
    )
    p = own
    opposite = n % 2 == 0 and n > 1
    rounds = (n - 1) // 2

    _, x_hbm, w_hbm = tie((own, requests, key_base_weight))
    x, there = call(
        base_kernel,
        [((rows, half), jnp.bfloat16), ((rows, out_keys), f32)],
        [HBM, HBM],
        x_hbm,
        w_hbm,
        mib=BASE_MIB,
        scratch=[
            pltpu.VMEM((half, out_keys), jnp.bfloat16),
            pltpu.SemaphoreType.DMA((BASE_STEPS,)),
            pltpu.SemaphoreType.DMA((BASE_STEPS,)),
        ],
    )
    there, q = tie((there, own))
    from_there = lax.ppermute(there, "tensor", swap)
    here = call(
        here_kernel,
        [((rows, out_keys), f32)],
        [VMEM, HBM],
        tie((there, x))[1],
        key_base_weight,
        mib=BASE_MIB,
        scratch=[pltpu.VMEM((half, out_keys), jnp.bfloat16), pltpu.SemaphoreType.DMA((BASE_STEPS,))],
    )

    def far_of(index):
        kernel = functools.partial(far_kernel, n)
        return call(kernel, [((rows, LANES), jnp.int32)], [VMEM, SMEM], index, storage_slot_index)

    def down_of(message, s, *total):
        return call(
            functools.partial(down_kernel, s, len(message) - 1),
            [((rows, rank), f32)],
            [VMEM] * (2 + len(message) + len(total)),
            tie((*message, x))[-1],
            far,
            *message,
            *total,
        )

    total = None
    pieces = [(0, (own,))]
    for s in range(1, rounds + 1):
        halved = opposite and s == rounds and s > 1
        if halved:
            p = (lax.ppermute(p, both, forth),)
            q = tuple(lax.ppermute(h, both, back) for h in (q[rank:], q[:rank]))[::-1]
        else:
            p = (lax.ppermute(p, both, forth),)
            q = (lax.ppermute(q, both, back),)
        if s == 1:
            far = far_of(tie((there, adapter_index))[1])
            here, far, *p = tie((here, far, *p))
            total = down_of((own,), 0)
        else:
            total = down_of(pieces[-1][1], pieces[-1][0], total)
            total, *p = tie((total, *p))
        pieces.append((s, tuple(p)))
        if halved:
            pieces.append((n - s, tuple(q)))
            break
        total = down_of(pieces[-1][1], s, total)
        if s == min(2, rounds):
            from_there, *q = tie((from_there, *q))
        total, *q = tie((total, *q))
        pieces.append((n - s, tuple(q)))
        p, q = p[0], q[0]
    late = pieces[-2:] if opposite and rounds > 1 else []
    if late:
        pieces = pieces[:-2]
    if opposite:
        p = (p[0] if late else p)[:rank]
        q = q[1] if late else q[rank:]
        total, q = tie((total, q)) if late else (total, q)
        p = lax.ppermute(p, both, forth)
        q = lax.ppermute(q, both, back)
    if total is None:
        far = far_of(adapter_index)
        total = down_of((own,), 0)
    elif not late:
        total = down_of(pieces[-1][1], pieces[-1][0], total)
    other = lax.ppermute(total, "tensor", swap)
    messages = [m if n <= 16 else m[:, half // 2 :] for _, ms in pieces for m in ms]
    base = call(
        functools.partial(up_kernel, [s for s, _ in pieces], [len(ms) for _, ms in pieces]),
        [((rows, out_keys), f32)],
        [VMEM] * (5 + len(messages)),
        far,
        total,
        other,
        here,
        from_there,
        *messages,
        mib=32 if n > 16 else 16,
    )
    if not opposite:
        return base.astype(jnp.bfloat16)
    kept = []
    for i, (s, message) in enumerate(late):
        if i:
            base, *message = tie((base, *message))
        kept = [down_of(tuple(message), s, *kept)]
    base, p, *kept = tie((base, p, *kept))
    first = call(functools.partial(half_kernel, 0, n // 2), [((rows, rank), f32)], [VMEM] * 3, x, far, p)
    first, q = tie((first, q))
    total = call(
        functools.partial(half_kernel, 1, n // 2),
        [((rows, rank), f32)],
        [VMEM] * (4 + len(kept)),
        x,
        far,
        q,
        first,
        *kept,
    )
    other = lax.ppermute(total, "tensor", swap)
    late = late + [(n // 2, (p, q))]
    messages = [m for _, ms in late for m in ms]
    return call(
        functools.partial(last_kernel, [s for s, _ in late], [len(ms) for _, ms in late]),
        [((rows, out_keys), jnp.bfloat16)],
        [VMEM] * (4 + len(messages)),
        far,
        total,
        other,
        base,
        *messages,
    )


def solution(mesh):
    placed = (
        P(("groups", "dp"), "tensor"),
        P(("groups", "dp"), None),
        P("groups"),
        P("tensor", None),
        P(("groups", "dp"), "tensor", None),
        P(("groups", "dp"), None, None),
    )
    n = mesh.shape["dp"]
    return jax.shard_map(
        functools.partial(shards, n),
        mesh=mesh,
        in_specs=placed,
        out_specs=P(("groups", "dp"), "tensor"),
        check_vma=False,
    )
```

```python
import functools

import jax
import jax.numpy as jnp
from jax import lax
from jax.experimental import pallas as pl
from jax.experimental.pallas import tpu as pltpu
from jax.sharding import PartitionSpec as P

LANES = 128
BASE_STEPS = 8
BASE_MIB = 48
PACK_MIB = 60
tie = lax.optimization_barrier
VMEM = pl.BlockSpec(memory_space=pltpu.VMEM)
SMEM = pl.BlockSpec(memory_space=pltpu.SMEM)
HBM = pl.BlockSpec(memory_space=pl.ANY)


def snakes(n):
    return n % 2 == 0 and n <= 16


def ring_of(n):
    if snakes(n):
        return list(range(0, n, 2)) + list(range(n - 1, 0, -2))
    return list(range(n))


def place_in(n, i):
    return jnp.where(i % 2 == 0, i // 2, n - 1 - i // 2) if snakes(n) else i


def call(kernel, outs, in_specs, *args, mib=16, scratch=(), moved=1000, out_space=VMEM):
    shapes = [jax.ShapeDtypeStruct(shape, dtype) for shape, dtype in outs]
    got = pl.pallas_call(
        kernel,
        in_specs=in_specs,
        out_specs=[out_space] * len(outs),
        out_shape=shapes,
        scratch_shapes=scratch,
        compiler_params=pltpu.CompilerParams(vmem_limit_bytes=mib << 20),
        cost_estimate=pl.CostEstimate(flops=1000, bytes_accessed=moved, transcendentals=0),
    )(*args)
    return got[0] if len(outs) == 1 else got


def pack_kernel(a_ref, b_ref, o_ref, held, in_sems, out_sems):
    rank, half = a_ref.shape
    k_half, b_half = half // 2, o_ref.shape[1] - half // 2
    first = lax.axis_index("tensor") * (2 * b_half)
    arriving, leaving = [], []
    for i in range(2):
        rows = pl.ds(i * rank, rank)
        b_first = pl.multiple_of(first + i * b_half, b_half)
        pairs = [
            (a_ref.at[:, pl.ds(i * k_half, k_half)], held.at[rows, pl.ds(0, k_half)]),
            (b_ref.at[:, pl.ds(b_first, b_half)], held.at[rows, pl.ds(k_half, b_half)]),
        ]
        arriving.append([pltpu.make_async_copy(*pair, in_sems.at[2 * i + j]) for j, pair in enumerate(pairs)])
        leaving.append(pltpu.make_async_copy(held.at[rows, :], o_ref.at[rows, :], out_sems.at[i]))
    for copies in arriving:
        for c in copies:
            c.start()
    for i in range(2):
        for c in arriving[i]:
            c.wait()
        leaving[i].start()
    for c in leaving:
        c.wait()


def far_kernel(n, index_ref, storage_ref, o_ref):
    here = place_in(n, lax.axis_index("dp"))
    way = 1 - 2 * lax.axis_index("tensor")
    index = index_ref[...]

    def look(j, far):
        return jnp.where(index == j, lax.rem((here - place_in(n, storage_ref[j])) * way + n, n), far)

    far = lax.fori_loop(0, n, look, jnp.zeros_like(index))
    o_ref[...] = jnp.broadcast_to(far, o_ref.shape)


def base_kernel(x_hbm, w_hbm, x_ref, o_ref, w_ref, x_sems, w_sems):
    depth = x_hbm.shape[1] // BASE_STEPS
    keys = o_ref.shape[1]
    columns = pl.ds(pl.multiple_of((1 - lax.axis_index("tensor")) * keys, keys), keys)
    copies = []
    for i in range(BASE_STEPS):
        k = pl.ds(i * depth, depth)
        copies.append(
            (
                pltpu.make_async_copy(x_hbm.at[:, k], x_ref.at[:, k], x_sems.at[i]),
                pltpu.make_async_copy(w_hbm.at[k, columns], w_ref.at[k, :], w_sems.at[i]),
            )
        )
        for c in copies[-1]:
            c.start()
    for i in range(BASE_STEPS):
        k = pl.ds(i * depth, depth)
        for c in copies[i]:
            c.wait()
        product = jnp.dot(x_ref[:, k], w_ref[k, :], preferred_element_type=jnp.float32)
        o_ref[...] = product if i == 0 else o_ref[...] + product


def here_kernel(x_ref, w_hbm, o_ref, w_ref, w_sems):
    depth = x_ref.shape[1] // BASE_STEPS
    keys = o_ref.shape[1]
    columns = pl.ds(pl.multiple_of(lax.axis_index("tensor") * keys, keys), keys)
    copies = []
    for i in range(BASE_STEPS):
        k = pl.ds(i * depth, depth)
        copies.append(pltpu.make_async_copy(w_hbm.at[k, columns], w_ref.at[k, :], w_sems.at[i]))
        copies[-1].start()
    for i in range(BASE_STEPS):
        k = pl.ds(i * depth, depth)
        copies[i].wait()
        product = jnp.dot(x_ref[:, k], w_ref[k, :], preferred_element_type=jnp.float32)
        o_ref[...] = product if i == 0 else o_ref[...] + product


def halves_of(m_refs, rank):
    if len(m_refs) == 2:
        return m_refs
    return [m_refs[0].at[pl.ds(i * rank, rank), :] for i in range(2)]


def down_kernel(s, split, x_ref, far_ref, *rest):
    o_ref = rest[-1]
    rank = o_ref.shape[1]
    k_half = x_ref.shape[1] // 2
    m_refs = rest[: 1 + split]
    rest = rest[1 + split :]
    part = None
    for i, m_ref in enumerate(halves_of(m_refs, rank)):
        product = lax.dot_general(
            x_ref[:, i * k_half : (i + 1) * k_half],
            m_ref[:, :k_half],
            (((1,), (1,)), ((), ())),
            preferred_element_type=jnp.float32,
        )
        part = product if part is None else part + product
    kept = rest[0][...] if len(rest) > 1 else 0.0
    o_ref[...] = jnp.where(far_ref[:, :rank] == s, part, kept)


def half_kernel(i, s, x_ref, far_ref, m_ref, *rest):
    o_ref = rest[-1]
    k_half = x_ref.shape[1] // 2
    part = lax.dot_general(
        x_ref[:, i * k_half : (i + 1) * k_half],
        m_ref[:, :k_half],
        (((1,), (1,)), ((), ())),
        preferred_element_type=jnp.float32,
    )
    if i == 1:
        kept = rest[1][...] if len(rest) > 2 else 0.0
        part = jnp.where(far_ref[:, : part.shape[1]] == s, part + rest[0][...], kept)
        middle = part.shape[0] // 2
        part = jnp.concatenate([part[:middle], part[middle:]], axis=1)
    o_ref[...] = part


def lift(steps, far_ref, total, ups):
    high = total.astype(jnp.bfloat16)
    low = (total - high.astype(jnp.float32)).astype(jnp.bfloat16)
    rank = total.shape[1]
    far = far_ref[:, :rank]
    b_all = jnp.concatenate(ups, axis=0)
    out = None
    for part in (low, high):
        part = part.astype(jnp.float32)
        wide = jnp.concatenate([jnp.where(far == s, part, 0.0).astype(jnp.bfloat16) for s in steps], axis=1)
        product = jnp.dot(wide, b_all, preferred_element_type=jnp.float32)
        out = product if out is None else out + product
    return out


def ups_of(counts, refs, rank, keys):
    ups = []
    for count in counts:
        parts = halves_of(refs[:count], rank)
        refs = refs[count:]
        ups.append(jnp.concatenate([m[:, m.shape[1] - keys // 2 :] for m in parts], axis=1))
    return ups


def up_kernel(steps, counts, far_ref, own_ref, other_ref, here_ref, there_ref, *rest):
    o_ref = rest[-1]
    ups = ups_of(counts, rest[:-1], own_ref.shape[1], o_ref.shape[1])
    lifted = lift(steps, far_ref, own_ref[...] + other_ref[...], ups)
    o_ref[...] = here_ref[...] + there_ref[...] + lifted


def last_kernel(steps, counts, far_ref, own_ref, other_ref, base_ref, *rest):
    o_ref, held, sems = rest[-3:]
    rows, keys = held.shape
    rank = own_ref.shape[1] // 2
    ups = ups_of(counts, rest[:-3], rank, keys)
    total = own_ref[...] + other_ref[...]
    copies = []
    for i in range(2):
        part = pl.ds(i * (rows // 2), rows // 2)
        lifted = lift(steps, far_ref.at[part, :], total[:, i * rank : (i + 1) * rank], ups)
        held[part, :] = (base_ref[part, :] + lifted).astype(jnp.bfloat16)
        copies.append(pltpu.make_async_copy(held.at[part, :], o_ref.at[part, :], sems.at[i]))
        copies[-1].start()
    for c in copies:
        c.wait()


def shards(n, requests, adapter_index, storage_slot_index, key_base_weight, down_factor, up_factor):
    rows, half = requests.shape
    rank = down_factor.shape[2]
    keys = up_factor.shape[2]
    out_keys = keys // 2
    f32 = jnp.float32

    order = ring_of(n)
    forth, back = [], []
    for j in range(n):
        a, b = order[j], order[(j + 1) % n]
        forth += [(2 * a, 2 * b), (2 * b + 1, 2 * a + 1)]
        back += [(2 * b, 2 * a), (2 * a + 1, 2 * b + 1)]
    swap = [(0, 1), (1, 0)]
    both = ("dp", "tensor")

    own = call(
        pack_kernel,
        [((2 * rank, half // 2 + out_keys // 2), jnp.bfloat16)],
        [HBM, HBM],
        down_factor[0].T,
        up_factor[0],
        mib=PACK_MIB,
        scratch=[
            pltpu.VMEM((2 * rank, half // 2 + out_keys // 2), jnp.bfloat16),
            pltpu.SemaphoreType.DMA((4,)),
            pltpu.SemaphoreType.DMA((2,)),
        ],
        out_space=HBM,
    )
    p = own
    opposite = n % 2 == 0 and n > 1
    rounds = (n - 1) // 2

    _, x_hbm, w_hbm = tie((own, requests, key_base_weight))
    x, there = call(
        base_kernel,
        [((rows, half), jnp.bfloat16), ((rows, out_keys), f32)],
        [HBM, HBM],
        x_hbm,
        w_hbm,
        mib=BASE_MIB,
        scratch=[
            pltpu.VMEM((half, out_keys), jnp.bfloat16),
            pltpu.SemaphoreType.DMA((BASE_STEPS,)),
            pltpu.SemaphoreType.DMA((BASE_STEPS,)),
        ],
    )
    there, q = tie((there, own))
    from_there = lax.ppermute(there, "tensor", swap)
    here = call(
        here_kernel,
        [((rows, out_keys), f32)],
        [VMEM, HBM],
        tie((there, x))[1],
        key_base_weight,
        mib=BASE_MIB,
        scratch=[pltpu.VMEM((half, out_keys), jnp.bfloat16), pltpu.SemaphoreType.DMA((BASE_STEPS,))],
    )

    def far_of(index):
        kernel = functools.partial(far_kernel, n)
        return call(kernel, [((rows, LANES), jnp.int32)], [VMEM, SMEM], index, storage_slot_index)

    def down_of(message, s, *total):
        return call(
            functools.partial(down_kernel, s, len(message) - 1),
            [((rows, rank), f32)],
            [VMEM] * (2 + len(message) + len(total)),
            tie((*message, x))[-1],
            far,
            *message,
            *total,
        )

    total = None
    pieces = [(0, (own,))]
    for s in range(1, rounds + 1):
        halved = opposite and s == rounds and s > 1
        if halved:
            p = (lax.ppermute(p, both, forth),)
            q = tuple(lax.ppermute(h, both, back) for h in (q[rank:], q[:rank]))[::-1]
        else:
            p = (lax.ppermute(p, both, forth),)
            q = (lax.ppermute(q, both, back),)
        if s == 1:
            far = far_of(tie((there, adapter_index))[1])
            here, far, *p = tie((here, far, *p))
            total = down_of((own,), 0)
        else:
            total = down_of(pieces[-1][1], pieces[-1][0], total)
            total, *p = tie((total, *p))
        pieces.append((s, tuple(p)))
        if halved:
            pieces.append((n - s, tuple(q)))
            break
        total = down_of(pieces[-1][1], s, total)
        if s == min(2, rounds):
            from_there, *q = tie((from_there, *q))
        total, *q = tie((total, *q))
        pieces.append((n - s, tuple(q)))
        p, q = p[0], q[0]
    late = pieces[-2:] if opposite and rounds > 1 else []
    if late:
        pieces = pieces[:-2]
    if opposite:
        p = (p[0] if late else p)[:rank]
        q = q[1] if late else q[rank:]
        total, q = tie((total, q)) if late else (total, q)
        p = lax.ppermute(p, both, forth)
        q = lax.ppermute(q, both, back)
    if total is None:
        far = far_of(adapter_index)
        total = down_of((own,), 0)
    elif not late:
        total = down_of(pieces[-1][1], pieces[-1][0], total)
    other = lax.ppermute(total, "tensor", swap)
    messages = [m if n <= 16 else m[:, half // 2 :] for _, ms in pieces for m in ms]
    base = call(
        functools.partial(up_kernel, [s for s, _ in pieces], [len(ms) for _, ms in pieces]),
        [((rows, out_keys), f32)],
        [VMEM] * (5 + len(messages)),
        far,
        total,
        other,
        here,
        from_there,
        *messages,
        mib=32 if n > 16 else 16,
    )
    if not opposite:
        return base.astype(jnp.bfloat16)
    kept = []
    for i, (s, message) in enumerate(late):
        if i:
            base, *message = tie((base, *message))
        kept = [down_of(tuple(message), s, *kept)]
    base, p, *kept = tie((base, p, *kept))
    first = call(functools.partial(half_kernel, 0, n // 2), [((rows, rank), f32)], [VMEM] * 3, x, far, p)
    first, q = tie((first, q))
    total = call(
        functools.partial(half_kernel, 1, n // 2),
        [((rows // 2, 2 * rank), f32)],
        [VMEM] * (4 + len(kept)),
        x,
        far,
        q,
        first,
        *kept,
    )
    other = lax.ppermute(total, "tensor", swap)
    late = late + [(n // 2, (p, q))]
    messages = [m for _, ms in late for m in ms]
    return call(
        functools.partial(last_kernel, [s for s, _ in late], [len(ms) for _, ms in late]),
        [((rows, out_keys), jnp.bfloat16)],
        [VMEM] * (4 + len(messages)),
        far,
        total,
        other,
        base,
        *messages,
        scratch=[pltpu.VMEM((rows, out_keys), jnp.bfloat16), pltpu.SemaphoreType.DMA((2,))],
        out_space=HBM,
    )


def solution(mesh):
    placed = (
        P(("groups", "dp"), "tensor"),
        P(("groups", "dp"), None),
        P("groups"),
        P("tensor", None),
        P(("groups", "dp"), "tensor", None),
        P(("groups", "dp"), None, None),
    )
    n = mesh.shape["dp"]
    return jax.shard_map(
        functools.partial(shards, n),
        mesh=mesh,
        in_specs=placed,
        out_specs=P(("groups", "dp"), "tensor"),
        check_vma=False,
    )
```

```python
import functools

import jax
import jax.numpy as jnp
from jax import lax
from jax.experimental import pallas as pl
from jax.experimental.pallas import tpu as pltpu
from jax.sharding import PartitionSpec as P

LANES = 128
BASE_STEPS = 8
BASE_MIB = 48
PACK_MIB = 60
tie = lax.optimization_barrier
VMEM = pl.BlockSpec(memory_space=pltpu.VMEM)
SMEM = pl.BlockSpec(memory_space=pltpu.SMEM)
HBM = pl.BlockSpec(memory_space=pl.ANY)


def snakes(n):
    return n % 2 == 0 and n <= 16


def ring_of(n):
    if snakes(n):
        return list(range(0, n, 2)) + list(range(n - 1, 0, -2))
    return list(range(n))


def place_in(n, i):
    return jnp.where(i % 2 == 0, i // 2, n - 1 - i // 2) if snakes(n) else i


def call(kernel, outs, in_specs, *args, mib=16, scratch=(), moved=1000, out_space=VMEM):
    shapes = [jax.ShapeDtypeStruct(shape, dtype) for shape, dtype in outs]
    got = pl.pallas_call(
        kernel,
        in_specs=in_specs,
        out_specs=[out_space] * len(outs),
        out_shape=shapes,
        scratch_shapes=scratch,
        compiler_params=pltpu.CompilerParams(vmem_limit_bytes=mib << 20),
        cost_estimate=pl.CostEstimate(flops=1000, bytes_accessed=moved, transcendentals=0),
    )(*args)
    return got[0] if len(outs) == 1 else got


def pack_kernel(a_ref, b_ref, o_ref, held, in_sems, out_sems):
    rank, half = a_ref.shape
    k_half, b_half = half // 2, o_ref.shape[1] - half // 2
    first = lax.axis_index("tensor") * (2 * b_half)
    arriving, leaving = [], []
    for i in range(2):
        rows = pl.ds(i * rank, rank)
        b_first = pl.multiple_of(first + i * b_half, b_half)
        pairs = [
            (a_ref.at[:, pl.ds(i * k_half, k_half)], held.at[rows, pl.ds(0, k_half)]),
            (b_ref.at[:, pl.ds(b_first, b_half)], held.at[rows, pl.ds(k_half, b_half)]),
        ]
        arriving.append([pltpu.make_async_copy(*pair, in_sems.at[2 * i + j]) for j, pair in enumerate(pairs)])
        leaving.append(pltpu.make_async_copy(held.at[rows, :], o_ref.at[rows, :], out_sems.at[i]))
    for copies in arriving:
        for c in copies:
            c.start()
    for i in range(2):
        for c in arriving[i]:
            c.wait()
        leaving[i].start()
    for c in leaving:
        c.wait()


def far_kernel(n, index_ref, storage_ref, o_ref):
    here = place_in(n, lax.axis_index("dp"))
    way = 1 - 2 * lax.axis_index("tensor")
    index = index_ref[...]

    def look(j, far):
        return jnp.where(index == j, lax.rem((here - place_in(n, storage_ref[j])) * way + n, n), far)

    far = lax.fori_loop(0, n, look, jnp.zeros_like(index))
    o_ref[...] = jnp.broadcast_to(far, o_ref.shape)


def base_kernel(x_hbm, w_hbm, x_ref, o_ref, w_ref, x_sems, w_sems):
    depth = x_hbm.shape[1] // BASE_STEPS
    keys = o_ref.shape[1]
    columns = pl.ds(pl.multiple_of((1 - lax.axis_index("tensor")) * keys, keys), keys)
    copies = []
    for i in range(BASE_STEPS):
        k = pl.ds(i * depth, depth)
        copies.append(
            (
                pltpu.make_async_copy(x_hbm.at[:, k], x_ref.at[:, k], x_sems.at[i]),
                pltpu.make_async_copy(w_hbm.at[k, columns], w_ref.at[k, :], w_sems.at[i]),
            )
        )
        for c in copies[-1]:
            c.start()
    for i in range(BASE_STEPS):
        k = pl.ds(i * depth, depth)
        for c in copies[i]:
            c.wait()
        product = jnp.dot(x_ref[:, k], w_ref[k, :], preferred_element_type=jnp.float32)
        o_ref[...] = product if i == 0 else o_ref[...] + product


def here_kernel(x_ref, w_hbm, o_ref, w_ref, w_sems):
    depth = x_ref.shape[1] // BASE_STEPS
    keys = o_ref.shape[1]
    columns = pl.ds(pl.multiple_of(lax.axis_index("tensor") * keys, keys), keys)
    copies = []
    for i in range(BASE_STEPS):
        k = pl.ds(i * depth, depth)
        copies.append(pltpu.make_async_copy(w_hbm.at[k, columns], w_ref.at[k, :], w_sems.at[i]))
        copies[-1].start()
    for i in range(BASE_STEPS):
        k = pl.ds(i * depth, depth)
        copies[i].wait()
        product = jnp.dot(x_ref[:, k], w_ref[k, :], preferred_element_type=jnp.float32)
        o_ref[...] = product if i == 0 else o_ref[...] + product


def halves_of(m_refs, rank):
    if len(m_refs) == 2:
        return m_refs
    return [m_refs[0].at[pl.ds(i * rank, rank), :] for i in range(2)]


def down_kernel(s, split, x_ref, far_ref, *rest):
    o_ref = rest[-1]
    rank = o_ref.shape[1]
    k_half = x_ref.shape[1] // 2
    m_refs = rest[: 1 + split]
    rest = rest[1 + split :]
    part = None
    for i, m_ref in enumerate(halves_of(m_refs, rank)):
        product = lax.dot_general(
            x_ref[:, i * k_half : (i + 1) * k_half],
            m_ref[:, :k_half],
            (((1,), (1,)), ((), ())),
            preferred_element_type=jnp.float32,
        )
        part = product if part is None else part + product
    kept = rest[0][...] if len(rest) > 1 else 0.0
    o_ref[...] = jnp.where(far_ref[:, :rank] == s, part, kept)


def half_kernel(i, s, x_ref, far_ref, m_ref, *rest):
    o_ref = rest[-1]
    k_half = x_ref.shape[1] // 2
    part = lax.dot_general(
        x_ref[:, i * k_half : (i + 1) * k_half],
        m_ref[:, :k_half],
        (((1,), (1,)), ((), ())),
        preferred_element_type=jnp.float32,
    )
    if i == 1:
        kept = rest[1][...] if len(rest) > 2 else 0.0
        part = jnp.where(far_ref[:, : part.shape[1]] == s, part + rest[0][...], kept)
        middle = part.shape[0] // 2
        part = jnp.concatenate([part[:middle], part[middle:]], axis=1)
    o_ref[...] = part


def lift(steps, far_ref, total, ups):
    high = total.astype(jnp.bfloat16)
    low = (total - high.astype(jnp.float32)).astype(jnp.bfloat16)
    rank = total.shape[1]
    far = far_ref[:, :rank]
    parts = [part.astype(jnp.float32) for part in (low, high)]
    wide = [jnp.where(far == s, part, 0.0).astype(jnp.bfloat16) for part in parts for s in steps]
    return jnp.dot(
        jnp.concatenate(wide, axis=1), jnp.concatenate(ups * 2, axis=0), preferred_element_type=jnp.float32
    )


def ups_of(counts, refs, rank, keys):
    ups = []
    for count in counts:
        parts = halves_of(refs[:count], rank)
        refs = refs[count:]
        ups.append(jnp.concatenate([m[:, m.shape[1] - keys // 2 :] for m in parts], axis=1))
    return ups


def up_kernel(steps, counts, far_ref, own_ref, other_ref, here_ref, there_ref, *rest):
    o_ref = rest[-1]
    ups = ups_of(counts, rest[:-1], own_ref.shape[1], o_ref.shape[1])
    lifted = lift(steps, far_ref, own_ref[...] + other_ref[...], ups)
    o_ref[...] = here_ref[...] + there_ref[...] + lifted


def last_kernel(steps, counts, far_ref, own_ref, other_ref, base_ref, *rest):
    o_ref, held, sems = rest[-3:]
    rows, keys = held.shape
    rank = own_ref.shape[1] // 2
    ups = ups_of(counts, rest[:-3], rank, keys)
    total = own_ref[...] + other_ref[...]
    copies = []
    deep = rows // 4
    for i in range(4):
        part = pl.ds(i * deep, deep)
        at, side = i % 2 * deep, i // 2 * rank
        lifted = lift(steps, far_ref.at[part, :], total[at : at + deep, side : side + rank], ups)
        held[part, :] = (base_ref[part, :] + lifted).astype(jnp.bfloat16)
        copies.append(pltpu.make_async_copy(held.at[part, :], o_ref.at[part, :], sems.at[i]))
        copies[-1].start()
    for c in copies:
        c.wait()


def shards(n, requests, adapter_index, storage_slot_index, key_base_weight, down_factor, up_factor):
    rows, half = requests.shape
    rank = down_factor.shape[2]
    keys = up_factor.shape[2]
    out_keys = keys // 2
    f32 = jnp.float32

    order = ring_of(n)
    forth, back = [], []
    for j in range(n):
        a, b = order[j], order[(j + 1) % n]
        forth += [(2 * a, 2 * b), (2 * b + 1, 2 * a + 1)]
        back += [(2 * b, 2 * a), (2 * a + 1, 2 * b + 1)]
    swap = [(0, 1), (1, 0)]
    both = ("dp", "tensor")

    own = call(
        pack_kernel,
        [((2 * rank, half // 2 + out_keys // 2), jnp.bfloat16)],
        [HBM, HBM],
        down_factor[0].T,
        up_factor[0],
        mib=PACK_MIB,
        scratch=[
            pltpu.VMEM((2 * rank, half // 2 + out_keys // 2), jnp.bfloat16),
            pltpu.SemaphoreType.DMA((4,)),
            pltpu.SemaphoreType.DMA((2,)),
        ],
        out_space=HBM,
    )
    p = own
    opposite = n % 2 == 0 and n > 1
    rounds = (n - 1) // 2

    _, x_hbm, w_hbm = tie((own, requests, key_base_weight))
    x, there = call(
        base_kernel,
        [((rows, half), jnp.bfloat16), ((rows, out_keys), f32)],
        [HBM, HBM],
        x_hbm,
        w_hbm,
        mib=BASE_MIB,
        scratch=[
            pltpu.VMEM((half, out_keys), jnp.bfloat16),
            pltpu.SemaphoreType.DMA((BASE_STEPS,)),
            pltpu.SemaphoreType.DMA((BASE_STEPS,)),
        ],
    )
    there, q = tie((there, own))
    from_there = lax.ppermute(there, "tensor", swap)
    here = call(
        here_kernel,
        [((rows, out_keys), f32)],
        [VMEM, HBM],
        tie((there, x))[1],
        key_base_weight,
        mib=BASE_MIB,
        scratch=[pltpu.VMEM((half, out_keys), jnp.bfloat16), pltpu.SemaphoreType.DMA((BASE_STEPS,))],
    )

    def far_of(index):
        kernel = functools.partial(far_kernel, n)
        return call(kernel, [((rows, LANES), jnp.int32)], [VMEM, SMEM], index, storage_slot_index)

    def down_of(message, s, *total):
        return call(
            functools.partial(down_kernel, s, len(message) - 1),
            [((rows, rank), f32)],
            [VMEM] * (2 + len(message) + len(total)),
            tie((*message, x))[-1],
            far,
            *message,
            *total,
        )

    total = None
    pieces = [(0, (own,))]
    for s in range(1, rounds + 1):
        halved = opposite and s == rounds and s > 1
        if halved:
            p = (lax.ppermute(p, both, forth),)
            q = tuple(lax.ppermute(h, both, back) for h in (q[rank:], q[:rank]))[::-1]
        else:
            p = (lax.ppermute(p, both, forth),)
            q = (lax.ppermute(q, both, back),)
        if s == 1:
            far = far_of(tie((there, adapter_index))[1])
            here, far, *p = tie((here, far, *p))
            total = down_of((own,), 0)
        else:
            total = down_of(pieces[-1][1], pieces[-1][0], total)
            total, *p = tie((total, *p))
        pieces.append((s, tuple(p)))
        if halved:
            pieces.append((n - s, tuple(q)))
            break
        total = down_of(pieces[-1][1], s, total)
        if s == min(2, rounds):
            from_there, *q = tie((from_there, *q))
        total, *q = tie((total, *q))
        pieces.append((n - s, tuple(q)))
        p, q = p[0], q[0]
    late = pieces[-2:] if opposite and rounds > 1 else []
    if late:
        pieces = pieces[:-2]
    if opposite:
        p = (p[0] if late else p)[:rank]
        q = q[1] if late else q[rank:]
        total, q = tie((total, q)) if late else (total, q)
        p = lax.ppermute(p, both, forth)
        q = lax.ppermute(q, both, back)
    if total is None:
        far = far_of(adapter_index)
        total = down_of((own,), 0)
    elif not late:
        total = down_of(pieces[-1][1], pieces[-1][0], total)
    other = lax.ppermute(total, "tensor", swap)
    messages = [m if n <= 16 else m[:, half // 2 :] for _, ms in pieces for m in ms]
    base = call(
        functools.partial(up_kernel, [s for s, _ in pieces], [len(ms) for _, ms in pieces]),
        [((rows, out_keys), f32)],
        [VMEM] * (5 + len(messages)),
        far,
        total,
        other,
        here,
        from_there,
        *messages,
        mib=32 if n > 16 else 16,
    )
    if not opposite:
        return base.astype(jnp.bfloat16)
    kept = []
    for i, (s, message) in enumerate(late):
        if i:
            base, *message = tie((base, *message))
        kept = [down_of(tuple(message), s, *kept)]
    base, p, *kept = tie((base, p, *kept))
    first = call(functools.partial(half_kernel, 0, n // 2), [((rows, rank), f32)], [VMEM] * 3, x, far, p)
    first, q = tie((first, q))
    total = call(
        functools.partial(half_kernel, 1, n // 2),
        [((rows // 2, 2 * rank), f32)],
        [VMEM] * (4 + len(kept)),
        x,
        far,
        q,
        first,
        *kept,
    )
    other = lax.ppermute(total, "tensor", swap)
    late = late + [(n // 2, (p, q))]
    messages = [m for _, ms in late for m in ms]
    return call(
        functools.partial(last_kernel, [s for s, _ in late], [len(ms) for _, ms in late]),
        [((rows, out_keys), jnp.bfloat16)],
        [VMEM] * (4 + len(messages)),
        far,
        total,
        other,
        base,
        *messages,
        scratch=[pltpu.VMEM((rows, out_keys), jnp.bfloat16), pltpu.SemaphoreType.DMA((4,))],
        out_space=HBM,
    )


def solution(mesh):
    placed = (
        P(("groups", "dp"), "tensor"),
        P(("groups", "dp"), None),
        P("groups"),
        P("tensor", None),
        P(("groups", "dp"), "tensor", None),
        P(("groups", "dp"), None, None),
    )
    n = mesh.shape["dp"]
    return jax.shard_map(
        functools.partial(shards, n),
        mesh=mesh,
        in_specs=placed,
        out_specs=P(("groups", "dp"), "tensor"),
        check_vma=False,
    )
```

```python
import functools

import jax
import jax.numpy as jnp
from jax import lax
from jax.experimental import pallas as pl
from jax.experimental.pallas import tpu as pltpu
from jax.sharding import PartitionSpec as P

LANES = 128
BASE_STEPS = 8
BASE_MIB = 48
PACK_MIB = 60
tie = lax.optimization_barrier
VMEM = pl.BlockSpec(memory_space=pltpu.VMEM)
SMEM = pl.BlockSpec(memory_space=pltpu.SMEM)
HBM = pl.BlockSpec(memory_space=pl.ANY)


def snakes(n):
    return n % 2 == 0 and n <= 16


def ring_of(n):
    if snakes(n):
        return list(range(0, n, 2)) + list(range(n - 1, 0, -2))
    return list(range(n))


def place_in(n, i):
    return jnp.where(i % 2 == 0, i // 2, n - 1 - i // 2) if snakes(n) else i


def call(kernel, outs, in_specs, *args, mib=16, scratch=(), moved=1000, out_space=VMEM):
    shapes = [jax.ShapeDtypeStruct(shape, dtype) for shape, dtype in outs]
    got = pl.pallas_call(
        kernel,
        in_specs=in_specs,
        out_specs=[out_space] * len(outs),
        out_shape=shapes,
        scratch_shapes=scratch,
        compiler_params=pltpu.CompilerParams(vmem_limit_bytes=mib << 20),
        cost_estimate=pl.CostEstimate(flops=1000, bytes_accessed=moved, transcendentals=0),
    )(*args)
    return got[0] if len(outs) == 1 else got


def pack_kernel(a_ref, b_ref, o_ref, held, in_sems, out_sems):
    rank, half = a_ref.shape
    k_half, b_half = half // 2, o_ref.shape[1] - half // 2
    first = lax.axis_index("tensor") * (2 * b_half)
    arriving, leaving = [], []
    for i in range(2):
        rows = pl.ds(i * rank, rank)
        b_first = pl.multiple_of(first + i * b_half, b_half)
        pairs = [
            (a_ref.at[:, pl.ds(i * k_half, k_half)], held.at[rows, pl.ds(0, k_half)]),
            (b_ref.at[:, pl.ds(b_first, b_half)], held.at[rows, pl.ds(k_half, b_half)]),
        ]
        arriving.append([pltpu.make_async_copy(*pair, in_sems.at[2 * i + j]) for j, pair in enumerate(pairs)])
        leaving.append(pltpu.make_async_copy(held.at[rows, :], o_ref.at[rows, :], out_sems.at[i]))
    for copies in arriving:
        for c in copies:
            c.start()
    for i in range(2):
        for c in arriving[i]:
            c.wait()
        leaving[i].start()
    for c in leaving:
        c.wait()


def far_kernel(n, index_ref, storage_ref, o_ref):
    here = place_in(n, lax.axis_index("dp"))
    way = 2 * lax.axis_index("tensor") - 1
    index = index_ref[...]

    def look(j, far):
        return jnp.where(index == j, lax.rem((here - place_in(n, storage_ref[j])) * way + n, n), far)

    far = lax.fori_loop(0, n, look, jnp.zeros_like(index))
    o_ref[...] = jnp.broadcast_to(far, o_ref.shape)


def base_kernel(x_hbm, w_hbm, x_ref, o_ref, w_ref, x_sems, w_sems):
    depth = x_hbm.shape[1] // BASE_STEPS
    keys = o_ref.shape[1]
    columns = pl.ds(pl.multiple_of((1 - lax.axis_index("tensor")) * keys, keys), keys)
    copies = []
    for i in range(BASE_STEPS):
        k = pl.ds(i * depth, depth)
        copies.append(
            (
                pltpu.make_async_copy(x_hbm.at[:, k], x_ref.at[:, k], x_sems.at[i]),
                pltpu.make_async_copy(w_hbm.at[k, columns], w_ref.at[k, :], w_sems.at[i]),
            )
        )
        for c in copies[-1]:
            c.start()
    for i in range(BASE_STEPS):
        k = pl.ds(i * depth, depth)
        for c in copies[i]:
            c.wait()
        product = jnp.dot(x_ref[:, k], w_ref[k, :], preferred_element_type=jnp.float32)
        o_ref[...] = product if i == 0 else o_ref[...] + product


def here_kernel(x_ref, w_hbm, o_ref, w_ref, w_sems):
    depth = x_ref.shape[1] // BASE_STEPS
    keys = o_ref.shape[1]
    columns = pl.ds(pl.multiple_of(lax.axis_index("tensor") * keys, keys), keys)
    copies = []
    for i in range(BASE_STEPS):
        k = pl.ds(i * depth, depth)
        copies.append(pltpu.make_async_copy(w_hbm.at[k, columns], w_ref.at[k, :], w_sems.at[i]))
        copies[-1].start()
    for i in range(BASE_STEPS):
        k = pl.ds(i * depth, depth)
        copies[i].wait()
        product = jnp.dot(x_ref[:, k], w_ref[k, :], preferred_element_type=jnp.float32)
        o_ref[...] = product if i == 0 else o_ref[...] + product


def halves_of(m_refs, rank):
    if len(m_refs) == 2:
        return m_refs
    return [m_refs[0].at[pl.ds(i * rank, rank), :] for i in range(2)]


def down_kernel(s, split, x_ref, far_ref, *rest):
    o_ref = rest[-1]
    rank = o_ref.shape[1]
    k_half = x_ref.shape[1] // 2
    m_refs = rest[: 1 + split]
    rest = rest[1 + split :]
    part = None
    for i, m_ref in enumerate(halves_of(m_refs, rank)):
        product = lax.dot_general(
            x_ref[:, i * k_half : (i + 1) * k_half],
            m_ref[:, :k_half],
            (((1,), (1,)), ((), ())),
            preferred_element_type=jnp.float32,
        )
        part = product if part is None else part + product
    kept = rest[0][...] if len(rest) > 1 else 0.0
    o_ref[...] = jnp.where(far_ref[:, :rank] == s, part, kept)


def half_kernel(i, s, x_ref, far_ref, m_ref, *rest):
    o_ref = rest[-1]
    k_half = x_ref.shape[1] // 2
    part = lax.dot_general(
        x_ref[:, i * k_half : (i + 1) * k_half],
        m_ref[:, :k_half],
        (((1,), (1,)), ((), ())),
        preferred_element_type=jnp.float32,
    )
    if i == 1:
        kept = rest[1][...] if len(rest) > 2 else 0.0
        part = jnp.where(far_ref[:, : part.shape[1]] == s, part + rest[0][...], kept)
        middle = part.shape[0] // 2
        part = jnp.concatenate([part[:middle], part[middle:]], axis=1)
    o_ref[...] = part


def lift(steps, far_ref, total, ups):
    high = total.astype(jnp.bfloat16)
    low = (total - high.astype(jnp.float32)).astype(jnp.bfloat16)
    rank = total.shape[1]
    far = far_ref[:, :rank]
    parts = [part.astype(jnp.float32) for part in (low, high)]
    wide = [jnp.where(far == s, part, 0.0).astype(jnp.bfloat16) for part in parts for s in steps]
    return jnp.dot(
        jnp.concatenate(wide, axis=1), jnp.concatenate(ups * 2, axis=0), preferred_element_type=jnp.float32
    )


def ups_of(counts, refs, rank, keys):
    ups = []
    for count in counts:
        parts = halves_of(refs[:count], rank)
        refs = refs[count:]
        ups.append(jnp.concatenate([m[:, m.shape[1] - keys // 2 :] for m in parts], axis=1))
    return ups


def up_kernel(steps, counts, far_ref, own_ref, other_ref, here_ref, there_ref, *rest):
    o_ref = rest[-1]
    ups = ups_of(counts, rest[:-1], own_ref.shape[1], o_ref.shape[1])
    lifted = lift(steps, far_ref, own_ref[...] + other_ref[...], ups)
    o_ref[...] = here_ref[...] + there_ref[...] + lifted


def last_kernel(steps, counts, far_ref, own_ref, other_ref, base_ref, *rest):
    o_ref, held, sems = rest[-3:]
    rows, keys = held.shape
    rank = own_ref.shape[1] // 2
    ups = ups_of(counts, rest[:-3], rank, keys)
    total = own_ref[...] + other_ref[...]
    copies = []
    deep = rows // 4
    for i in range(4):
        part = pl.ds(i * deep, deep)
        at, side = i % 2 * deep, i // 2 * rank
        lifted = lift(steps, far_ref.at[part, :], total[at : at + deep, side : side + rank], ups)
        held[part, :] = (base_ref[part, :] + lifted).astype(jnp.bfloat16)
        copies.append(pltpu.make_async_copy(held.at[part, :], o_ref.at[part, :], sems.at[i]))
        copies[-1].start()
    for c in copies:
        c.wait()


def shards(n, requests, adapter_index, storage_slot_index, key_base_weight, down_factor, up_factor):
    rows, half = requests.shape
    rank = down_factor.shape[2]
    keys = up_factor.shape[2]
    out_keys = keys // 2
    f32 = jnp.float32

    order = ring_of(n)
    forth, back = [], []
    for j in range(n):
        a, b = order[j], order[(j + 1) % n]
        back += [(2 * a, 2 * b), (2 * b + 1, 2 * a + 1)]
        forth += [(2 * b, 2 * a), (2 * a + 1, 2 * b + 1)]
    swap = [(0, 1), (1, 0)]
    both = ("dp", "tensor")

    own = call(
        pack_kernel,
        [((2 * rank, half // 2 + out_keys // 2), jnp.bfloat16)],
        [HBM, HBM],
        down_factor[0].T,
        up_factor[0],
        mib=PACK_MIB,
        scratch=[
            pltpu.VMEM((2 * rank, half // 2 + out_keys // 2), jnp.bfloat16),
            pltpu.SemaphoreType.DMA((4,)),
            pltpu.SemaphoreType.DMA((2,)),
        ],
        out_space=HBM,
    )
    p = own
    opposite = n % 2 == 0 and n > 1
    rounds = (n - 1) // 2

    _, x_hbm, w_hbm = tie((own, requests, key_base_weight))
    x, there = call(
        base_kernel,
        [((rows, half), jnp.bfloat16), ((rows, out_keys), f32)],
        [HBM, HBM],
        x_hbm,
        w_hbm,
        mib=BASE_MIB,
        scratch=[
            pltpu.VMEM((half, out_keys), jnp.bfloat16),
            pltpu.SemaphoreType.DMA((BASE_STEPS,)),
            pltpu.SemaphoreType.DMA((BASE_STEPS,)),
        ],
    )
    there, q = tie((there, own))
    from_there = lax.ppermute(there, "tensor", swap)
    here = call(
        here_kernel,
        [((rows, out_keys), f32)],
        [VMEM, HBM],
        tie((there, x))[1],
        key_base_weight,
        mib=BASE_MIB,
        scratch=[pltpu.VMEM((half, out_keys), jnp.bfloat16), pltpu.SemaphoreType.DMA((BASE_STEPS,))],
    )

    def far_of(index):
        kernel = functools.partial(far_kernel, n)
        return call(kernel, [((rows, LANES), jnp.int32)], [VMEM, SMEM], index, storage_slot_index)

    def down_of(message, s, *total):
        return call(
            functools.partial(down_kernel, s, len(message) - 1),
            [((rows, rank), f32)],
            [VMEM] * (2 + len(message) + len(total)),
            tie((*message, x))[-1],
            far,
            *message,
            *total,
        )

    total = None
    pieces = [(0, (own,))]
    for s in range(1, rounds + 1):
        halved = opposite and s == rounds and s > 1
        if halved:
            p = (lax.ppermute(p, both, forth),)
            q = tuple(lax.ppermute(h, both, back) for h in (q[rank:], q[:rank]))[::-1]
        else:
            p = (lax.ppermute(p, both, forth),)
            q = (lax.ppermute(q, both, back),)
        if s == 1:
            far = far_of(tie((there, adapter_index))[1])
            here, far, *p = tie((here, far, *p))
            total = down_of((own,), 0)
        else:
            total = down_of(pieces[-1][1], pieces[-1][0], total)
            total, *p = tie((total, *p))
        pieces.append((s, tuple(p)))
        if halved:
            pieces.append((n - s, tuple(q)))
            break
        total = down_of(pieces[-1][1], s, total)
        if s == min(2, rounds):
            from_there, *q = tie((from_there, *q))
        total, *q = tie((total, *q))
        pieces.append((n - s, tuple(q)))
        p, q = p[0], q[0]
    late = pieces[-2:] if opposite and rounds > 1 else []
    if late:
        pieces = pieces[:-2]
    if opposite:
        p = (p[0] if late else p)[:rank]
        q = q[1] if late else q[rank:]
        total, q = tie((total, q)) if late else (total, q)
        p = lax.ppermute(p, both, forth)
        q = lax.ppermute(q, both, back)
    if total is None:
        far = far_of(adapter_index)
        total = down_of((own,), 0)
    elif not late:
        total = down_of(pieces[-1][1], pieces[-1][0], total)
    other = lax.ppermute(total, "tensor", swap)
    messages = [m if n <= 16 else m[:, half // 2 :] for _, ms in pieces for m in ms]
    base = call(
        functools.partial(up_kernel, [s for s, _ in pieces], [len(ms) for _, ms in pieces]),
        [((rows, out_keys), f32)],
        [VMEM] * (5 + len(messages)),
        far,
        total,
        other,
        here,
        from_there,
        *messages,
        mib=32 if n > 16 else 16,
    )
    if not opposite:
        return base.astype(jnp.bfloat16)
    kept = []
    for i, (s, message) in enumerate(late):
        if i:
            base, *message = tie((base, *message))
        kept = [down_of(tuple(message), s, *kept)]
    base, p, *kept = tie((base, p, *kept))
    first = call(functools.partial(half_kernel, 0, n // 2), [((rows, rank), f32)], [VMEM] * 3, x, far, p)
    first, q = tie((first, q))
    total = call(
        functools.partial(half_kernel, 1, n // 2),
        [((rows // 2, 2 * rank), f32)],
        [VMEM] * (4 + len(kept)),
        x,
        far,
        q,
        first,
        *kept,
    )
    other = lax.ppermute(total, "tensor", swap)
    late = late + [(n // 2, (p, q))]
    messages = [m for _, ms in late for m in ms]
    return call(
        functools.partial(last_kernel, [s for s, _ in late], [len(ms) for _, ms in late]),
        [((rows, out_keys), jnp.bfloat16)],
        [VMEM] * (4 + len(messages)),
        far,
        total,
        other,
        base,
        *messages,
        scratch=[pltpu.VMEM((rows, out_keys), jnp.bfloat16), pltpu.SemaphoreType.DMA((4,))],
        out_space=HBM,
    )


def solution(mesh):
    placed = (
        P(("groups", "dp"), "tensor"),
        P(("groups", "dp"), None),
        P("groups"),
        P("tensor", None),
        P(("groups", "dp"), "tensor", None),
        P(("groups", "dp"), None, None),
    )
    n = mesh.shape["dp"]
    return jax.shard_map(
        functools.partial(shards, n),
        mesh=mesh,
        in_specs=placed,
        out_specs=P(("groups", "dp"), "tensor"),
        check_vma=False,
    )
```
